256 devices in a mesh: row: 8 (over y, x_lo), col: 32 (over x_hi, z, core).
Axes of the slice: x: 4 (x_hi: 2, x_lo: 2; x = x_hi * 2 + x_lo), y: 4, z: 8, core: 2. Of those that a mesh axis runs over, the one named last changes fastest.
Arguments:
- out_grad: bfloat16 [65536, 256], P(('row', 'col')), may hold values from -6 to 6
- pre_act: bfloat16 [65536, 256], P(('row', 'col')), may hold values from -6 to 6
- features: bfloat16 [65536, 256], P(('col', 'row')), may hold values from -0.119628906 to 0.119628906
- weight: bfloat16 [256, 256], replicated, may hold values from -0.375 to 0.375
- inv_degree: float32 [65536], replicated, may hold values from 0.01 to 0.2
- node_time: int32 [65536], replicated, may hold values from 0 to 31
- decay_rate: float32 [1], replicated, may hold values from 0.03 to 0.15
- tile_value: bfloat16 [8, 5632, 128, 128], P('row', 'col'), may hold values from 0 to 1
- tile_row: int32 [8, 5632], P('row', 'col'), may hold values from 0 to 63, as said below
- tile_col: int32 [8, 5632], P('row', 'col'), may hold values from 0 to 15
- tile_count: int32 [8, 32], P('row', 'col'), may hold values from 1 to 176, as said below
Outputs:
- grad_input: bfloat16 [65536, 256], P(('col', 'row'))
- weight_grad: float32 [256, 256], replicated
The draws below stay inside these ranges and needn't reach their ends.
Inputs may be any that keep to these rules, and one draw needn't show every extreme that they name: `tile_count`: some block has exactly 176 live slots in every draw. `tile_row`: in each block the live slots (the first tile_count) name distinct tiles, in increasing order of tile row and then tile column; slots from tile_count on name arbitrary tiles.
All inputs are finite; a program needn't handle non-finite values.
Results may differ from the reference program's by a relative error of at most 0.0058.
Values may be sent and summed in bfloat16 or wider, within the bound.
No kernel may reach another device: no remote copies, remote signals or barrier semaphores. Data moves between devices by JAX's collectives and lax.ppermute only.
A program may use at most 64 MiB of HBM per device.

```python
import math
import jax
import jax.numpy as jnp
from jax import lax

F_IN = 256
F_OUT = 256
TILE = 128
TIME_BUCKETS = 32
NODE_DEV = 256
NODES = 65536
TILE_ROWS = 64
TILE_COLS = 16
SLOTS = 176
N_ROW = 8
N_COL = 32


def tile_layout(key):
    devices = N_ROW * N_COL
    tile_grid = TILE_ROWS * TILE_COLS
    key_load, key_busy, key_pick = jax.random.split(key, 3)
    load_level = jax.random.randint(key_load, (devices,), 1, 17)
    busiest = jax.random.randint(key_busy, (), 0, devices)
    load_level = jnp.where(jnp.arange(devices) == busiest, 16, load_level)
    live_count = jnp.maximum(SLOTS * load_level * load_level // 256, 1)
    picked = jax.vmap(lambda single: jax.random.permutation(single, tile_grid)[:SLOTS])(jax.random.split(key_pick, devices))
    slot_index = jnp.arange(SLOTS)
    sort_key = jnp.where(slot_index[None, :] < live_count[:, None], picked, picked + tile_grid)
    position = jnp.sort(sort_key, axis=1) % tile_grid
    return (position.astype(jnp.int32), live_count.astype(jnp.int32))


def draw_tile_row(key, part):
    position, live_count = tile_layout(key)
    return (position // TILE_COLS).reshape(N_ROW, N_COL * SLOTS).astype(jnp.int32)


def draw_tile_col(key, part):
    position, live_count = tile_layout(key)
    return (position % TILE_COLS).reshape(N_ROW, N_COL * SLOTS).astype(jnp.int32)


def draw_tile_count(key, part):
    position, live_count = tile_layout(key)
    return live_count.reshape(N_ROW, N_COL).astype(jnp.int32)


def set_ends(values, key, least, top_value):
    index_at = [jax.random.randint(jax.random.fold_in(key, axis), (), 0, length) for axis, length in enumerate(values.shape)]
    main_axis = values.shape.index(max(values.shape))
    neighbour = index_at[:main_axis] + [(index_at[main_axis] + 1) % values.shape[main_axis]] + index_at[main_axis + 1:]
    return values.at[tuple(index_at)].set(least).at[tuple(neighbour)].set(top_value)


def levels(rng, extent, shards, low, top_value):
    def one(dim, blocks):
        heights = jax.random.uniform(jax.random.fold_in(jax.random.fold_in(rng, 6), dim), (blocks,), jnp.float32, low / len(shards), top_value / len(shards))
        return jnp.repeat(jnp.exp(heights), extent[dim] // blocks).reshape((-1,) + (1,) * (len(extent) - dim - 1))

    loudness = one(*shards[0])
    for cut in shards[1:]:
        loudness = loudness * one(*cut)
    return loudness


def bell_draw(rng, shape, width, most, shards=(), held_as=jnp.bfloat16):
    loudness = levels(rng, shape, shards, -0.22, 0.18) if shards else 1.0
    values = jax.random.normal(rng, shape, jnp.float32) * width * loudness
    return jnp.minimum(jnp.maximum(values, -most), most).astype(held_as)


def setup_inputs(seed: int = 0) -> dict:
    key_list = jax.random.split(jax.random.key(seed), 12)
    return {
        "out_grad": bell_draw(key_list[0], (NODES, F_OUT), 1.0, 6.0, ((0, 256),)),
        "pre_act": bell_draw(key_list[1], (NODES, F_OUT), 1.0, 6.0, ((0, 256),)),
        "features": bell_draw(key_list[2], (NODES, F_IN), 0.02, 0.119628906, ((0, 256),)),
        "weight": bell_draw(key_list[3], (F_IN, F_OUT), F_OUT ** -0.5, 0.375),
        "inv_degree": jnp.clip(jnp.exp(jax.random.uniform(key_list[4], (NODES,), jnp.float32, math.log(0.01), math.log(0.2))), 0.01, 0.2),
        "node_time": set_ends(jax.random.randint(key_list[5], (NODES,), 0, TIME_BUCKETS), jax.random.fold_in(key_list[5], 1), 0, TIME_BUCKETS - 1).astype(jnp.int32),
        "decay_rate": jnp.clip(jax.random.uniform(key_list[6], (1,), jnp.float32, 0.03, 0.15), 0.03, 0.15),
        "tile_value": jnp.clip(1.0 * jax.random.uniform(key_list[7], (N_ROW, N_COL * SLOTS, TILE, TILE), jnp.float32) ** levels(key_list[7], (N_ROW, N_COL * SLOTS, TILE, TILE), ((0, 8), (1, 32)), -0.2, 0.2), 0.0, 1.0).astype(jnp.bfloat16),
        "tile_row": draw_tile_row(jax.random.fold_in(key_list[11], 71), 0),
        "tile_col": draw_tile_col(jax.random.fold_in(key_list[11], 71), 0),
        "tile_count": draw_tile_count(jax.random.fold_in(key_list[11], 71), 0),
    }


slot_block = 16


def edge_tiles(values, tile_rows, tile_cols, inside, row_times, col_times, row_scale, decay):
    tile_width = values.shape[2]
    offsets = jnp.arange(tile_width, dtype=jnp.int32)
    source_index = tile_rows[:, None] * tile_width + offsets[None, :]
    target_index = tile_cols[:, None] * tile_width + offsets[None, :]
    source_time = jnp.take(row_times, source_index, axis=0, mode="clip")
    target_time = jnp.take(col_times, target_index, axis=0, mode="clip")
    source_scale = jnp.take(row_scale, source_index, axis=0, mode="clip")
    time_gap = jnp.abs(target_time[:, None, :] - source_time[:, :, None]).astype(jnp.float32)
    edges = values.astype(jnp.float32) * jnp.exp(-decay * time_gap) * source_scale[:, :, None] * inside[:, None, None]
    return edges.astype(jnp.bfloat16)


def reference(out_grad, pre_act, features, weight, inv_degree, node_time, decay_rate, tile_value, tile_row, tile_col, tile_count):
    masked_grad = jnp.where(pre_act > 0, out_grad, jnp.zeros_like(out_grad))
    devices = N_ROW * N_COL
    rows_per_block = NODE_DEV * N_COL
    cols_per_block = NODE_DEV * N_ROW
    width_out = out_grad.shape[1]
    panels = masked_grad.reshape(NODES // TILE, TILE, width_out)
    values_all = tile_value.reshape(devices, SLOTS, TILE, TILE)
    rows_all = tile_row.reshape(devices, SLOTS)
    cols_all = tile_col.reshape(devices, SLOTS)
    counts_all = tile_count.reshape(devices)
    decay = decay_rate[0]

    def one_device(device, accum):
        device_index = jnp.asarray(device).astype(jnp.int32)
        row_index = device_index // N_COL
        col_index = device_index % N_COL
        row_times = lax.dynamic_slice_in_dim(node_time, row_index * rows_per_block, rows_per_block)
        col_times = lax.dynamic_slice_in_dim(node_time, col_index * cols_per_block, cols_per_block)
        row_scale = lax.dynamic_slice_in_dim(inv_degree, row_index * rows_per_block, rows_per_block)
        values = values_all[device_index]
        tile_rows = rows_all[device_index]
        tile_cols = cols_all[device_index]
        live_count = counts_all[device_index]

        def one_block(step_index, running):
            slot_start = jnp.asarray(step_index).astype(jnp.int32) * slot_block
            chosen = slot_start + jnp.arange(slot_block, dtype=jnp.int32)
            inside = (chosen < live_count).astype(jnp.float32)
            slot_rows = lax.dynamic_slice_in_dim(tile_rows, slot_start, slot_block, 0)
            slot_cols = lax.dynamic_slice_in_dim(tile_cols, slot_start, slot_block, 0)
            slot_values = lax.dynamic_slice_in_dim(values, slot_start, slot_block, 0)
            edges = edge_tiles(slot_values, slot_rows, slot_cols, inside, row_times, col_times, row_scale, decay)
            inputs = jnp.take(panels, row_index * TILE_ROWS + slot_rows, axis=0)
            contrib = jnp.einsum("bij,bif->bjf", edges.astype(jnp.float32), inputs.astype(jnp.float32))
            return running.at[col_index * TILE_COLS + slot_cols].add(contrib)

        return lax.fori_loop(0, (live_count + slot_block - 1) // slot_block, one_block, accum)

    summed = lax.fori_loop(0, devices, one_device, jnp.zeros((NODES // TILE, TILE, width_out), jnp.float32))
    summed = summed.reshape(NODES, width_out)
    node_grad = summed.astype(jnp.bfloat16)
    grad_input = jnp.dot(node_grad, weight.T, preferred_element_type=jnp.float32).astype(jnp.bfloat16)
    weight_grad = jnp.dot(features.astype(jnp.float32).T, summed, precision=lax.Precision.HIGHEST)
    return grad_input, weight_grad
```

```python
import jax
import jax.numpy as jnp
from jax import lax
from jax.experimental import pallas as pl
from jax.experimental.pallas import tpu as pltpu
from jax.sharding import Mesh, PartitionSpec as P

ROW = ("y", "xl")
COL = ("xh", "z", "c")
NEAR = ROW + ("c",)
FAR = ("xh", "z")
TILE = 128
CHUNK = 16
UNROLL = 8
VMEM = pl.BlockSpec(memory_space=pltpu.VMEM)
SMEM = pl.BlockSpec(memory_space=pltpu.SMEM)
ANY = pl.BlockSpec(memory_space=pl.ANY)
BIG = pltpu.CompilerParams(vmem_limit_bytes=48 << 20)
F32 = jnp.float32
BF16 = jnp.bfloat16


def mask_kernel(grad_ref, act_ref, feat_ref, out_ref, feat_t_ref):
    grad = grad_ref[...].astype(F32)
    kept = jnp.where(act_ref[...].astype(F32) > 0, grad, 0.0)
    out_ref[...] = kept.T.astype(BF16)
    feat_t_ref[...] = feat_ref[...].astype(F32).T.astype(BF16)


def edge_kernel(
    where_ref,
    rows_ref,
    cols_ref,
    count_ref,
    decay_ref,
    values_ref,
    time_ref,
    degree_ref,
    edge_ref,
    row_time,
    col_time,
    row_scale,
    near_row,
    far_row,
    near_col,
    far_col,
    value_sem,
    node_sem,
):
    slots = edge_ref.shape[0]
    chunks = slots // CHUNK
    tile_rows = row_time.shape[0]
    tile_cols = col_time.shape[0]
    row_at = pl.multiple_of(where_ref[0] * tile_rows, 8)
    col_at = pl.multiple_of(where_ref[1] * tile_cols, 8)
    node_copies = [
        pltpu.make_async_copy(
            time_ref.at[pl.ds(row_at, tile_rows)], row_time, node_sem.at[0]
        ),
        pltpu.make_async_copy(
            time_ref.at[pl.ds(col_at, tile_cols)], col_time, node_sem.at[1]
        ),
        pltpu.make_async_copy(
            degree_ref.at[pl.ds(row_at, tile_rows)], row_scale, node_sem.at[2]
        ),
    ]
    for copy in node_copies:
        copy.start()

    def value_copy(chunk):
        part = pl.ds(pl.multiple_of(chunk * CHUNK, CHUNK), CHUNK)
        return pltpu.make_async_copy(
            values_ref.at[0, part], edge_ref.at[part], value_sem.at[chunk]
        )

    for chunk in range(chunks):
        value_copy(chunk).start()
    for copy in node_copies:
        copy.wait()

    decay = decay_ref[0]
    count = count_ref[0, 0]
    later = decay * row_time[...].astype(F32)
    scale = row_scale[...]
    down = (jnp.exp(-later) * scale).T
    up = (jnp.exp(later) * scale).T
    for row in range(tile_rows):
        near_row[row] = jnp.broadcast_to(down[:, row : row + 1], (TILE, TILE))
        far_row[row] = jnp.broadcast_to(up[:, row : row + 1], (TILE, TILE))
    later = decay * col_time[...].astype(F32)
    near_col[...] = jnp.exp(later).reshape(tile_cols, 1, TILE)
    far_col[...] = jnp.exp(-later).reshape(tile_cols, 1, TILE)

    def one_chunk(chunk, carry):
        value_copy(chunk).wait()

        @pl.when(chunk * CHUNK < count)
        def _():
            for offset in range(CHUNK):
                slot = chunk * CHUNK + offset
                row = rows_ref[0, slot]
                col = cols_ref[0, slot]
                inside = jnp.where(slot < count, 1.0, 0.0).astype(F32)
                weight = jnp.minimum(
                    near_row[row] * (near_col[col] * inside),
                    far_row[row] * (far_col[col] * inside),
                )
                edge_ref[slot] = (edge_ref[slot].astype(F32) * weight).astype(BF16)

        return carry

    lax.fori_loop(0, chunks, one_chunk, 0)


def sum_kernel(n, ids_ref, rows_ref, cols_ref, count_ref, *refs):
    blocks = refs[:n]
    edge_ref, out_ref, panel, total = refs[n:]
    for k in range(n):
        at = ids_ref[k] * 2
        panel[at] = blocks[k][:, :TILE]
        panel[at + 1] = blocks[k][:, TILE:]
    total[...] = jnp.zeros_like(total)
    count = count_ref[0, 0]

    def group(index, carry):
        parts = []
        for offset in range(UNROLL):
            slot = index * UNROLL + offset
            parts.append(
                jnp.dot(
                    panel[rows_ref[0, slot]],
                    edge_ref[slot],
                    preferred_element_type=F32,
                )
            )
        for offset in range(UNROLL):
            total[cols_ref[0, index * UNROLL + offset]] += parts[offset]
        return carry

    lax.fori_loop(0, (count + UNROLL - 1) // UNROLL, group, 0)
    for col in range(total.shape[0]):
        half = (col % 2) * TILE
        out_ref[col // 2, :, half : half + TILE] = total[col].astype(BF16)


def finish_kernel(part_ref, feat_t_ref, weight_ref, input_ref, local_ref):
    summed = part_ref[0].astype(F32)
    for k in range(1, part_ref.shape[0]):
        summed = summed + part_ref[k].astype(F32)
    summed = summed.T
    high = summed.astype(BF16)
    low = (summed - high.astype(F32)).astype(BF16)
    input_ref[...] = lax.dot_general(
        high, weight_ref[...], (((1,), (1,)), ((), ())), preferred_element_type=F32
    ).astype(BF16)
    local = jnp.dot(feat_t_ref[...], high, preferred_element_type=F32) + jnp.dot(
        feat_t_ref[...], low, preferred_element_type=F32
    )
    local_ref[...] = local.reshape(local_ref.shape)


def spread_kernel(in_ref, out_ref):
    total = in_ref[0]
    for k in range(1, in_ref.shape[0]):
        total = total + in_ref[k]
    for k in range(out_ref.shape[0]):
        out_ref[k] = total


def shift(block, axis, step):
    size = lax.axis_size(axis)
    return lax.ppermute(block, axis, [(i, (i + step) % size) for i in range(size)])


def gather(own):
    ring = lax.axis_size("z")
    half = ring // 2
    blocks = []
    across = shift(own, "xh", 1)
    for flip, block in ((0, own), (1, across)):
        blocks.append((flip, 0, block))
        for sign in (1, -1):
            reach = half if (sign == 1) == (flip == 0) else half - 1
            moving = block
            for step in range(1, reach + 1):
                moving = shift(moving, "z", sign)
                blocks.append((flip, -sign * step, moving))
    found = []
    for flip, dz, block in blocks:
        found.append((flip, dz, 0, block))
        found.append((flip, dz, 1, shift(block, "c", 1)))
    return found


def shards(
    out_grad,
    pre_act,
    features,
    weight,
    inv_degree,
    node_time,
    decay_rate,
    tile_value,
    tile_row,
    tile_col,
    tile_count,
):
    nodes, width = out_grad.shape
    slots = tile_value.shape[1]
    n_row = lax.axis_size(ROW)
    n_col = lax.axis_size(COL)
    tile_rows = nodes * n_col // TILE
    tile_cols = nodes * n_row // TILE
    where = jnp.stack([lax.axis_index(ROW), lax.axis_index(COL)]).astype(jnp.int32)

    masked, features_t = pl.pallas_call(
        mask_kernel,
        out_shape=(
            jax.ShapeDtypeStruct((width, nodes), BF16),
            jax.ShapeDtypeStruct((features.shape[1], nodes), BF16),
        ),
        in_specs=[VMEM] * 3,
        out_specs=(VMEM, VMEM),
    )(out_grad, pre_act, features)

    found = gather(masked)

    edges = pl.pallas_call(
        edge_kernel,
        out_shape=jax.ShapeDtypeStruct((slots, TILE, TILE), BF16),
        in_specs=[SMEM] * 5 + [ANY] * 3,
        out_specs=VMEM,
        scratch_shapes=[
            pltpu.VMEM((tile_rows, TILE), jnp.int32),
            pltpu.VMEM((tile_cols, TILE), jnp.int32),
            pltpu.VMEM((tile_rows, TILE), F32),
            pltpu.VMEM((tile_rows, TILE, TILE), F32),
            pltpu.VMEM((tile_rows, TILE, TILE), F32),
            pltpu.VMEM((tile_cols, 1, TILE), F32),
            pltpu.VMEM((tile_cols, 1, TILE), F32),
            pltpu.SemaphoreType.DMA((slots // CHUNK,)),
            pltpu.SemaphoreType.DMA((3,)),
        ],
        compiler_params=BIG,
        cost_estimate=pl.CostEstimate(
            flops=6 * slots * TILE * TILE,
            bytes_accessed=4 * slots * TILE * TILE,
            transcendentals=0,
        ),
    )(
        where,
        tile_row,
        tile_col,
        tile_count,
        decay_rate,
        tile_value,
        node_time.reshape(-1, TILE),
        inv_degree.reshape(-1, TILE),
    )

    xh, z, c = (lax.axis_index(name) for name in COL)
    ids = jnp.stack(
        [
            ((xh ^ flip) * lax.axis_size("z") + ((z + dz) % lax.axis_size("z"))) * 2
            + (c ^ other)
            for flip, dz, other, _ in found
        ]
    ).astype(jnp.int32)
    blocks = [block for _, _, _, block in found]
    partial = pl.pallas_call(
        lambda *refs: sum_kernel(len(blocks), *refs),
        out_shape=jax.ShapeDtypeStruct((n_row, width, nodes), BF16),
        in_specs=[SMEM] * 4 + [VMEM] * (len(blocks) + 1),
        out_specs=VMEM,
        scratch_shapes=[
            pltpu.VMEM((tile_rows, width, TILE), BF16),
            pltpu.VMEM((tile_cols, width, TILE), F32),
        ],
        compiler_params=BIG,
    )(ids, tile_row, tile_col, tile_count, *blocks, edges)

    parts = lax.all_to_all(partial, ROW, 0, 0, tiled=True)

    n_near = lax.axis_size(NEAR)
    n_far = lax.axis_size(FAR)
    part_rows = features.shape[1] // n_near
    grad_input, local = pl.pallas_call(
        finish_kernel,
        out_shape=(
            jax.ShapeDtypeStruct((nodes, features.shape[1]), BF16),
            jax.ShapeDtypeStruct((n_near, part_rows, width), F32),
        ),
        in_specs=[VMEM] * 3,
        out_specs=(VMEM, VMEM),
    )(parts, features_t, weight)

    def spread(array, copies):
        return pl.pallas_call(
            spread_kernel,
            out_shape=jax.ShapeDtypeStruct((copies,) + array.shape[1:], F32),
            in_specs=[VMEM],
            out_specs=VMEM,
        )(array)

    slices = lax.all_to_all(local, NEAR, 0, 0, tiled=True)
    slices = lax.all_to_all(spread(slices, n_far), FAR, 0, 0, tiled=True)
    slices = lax.all_to_all(spread(slices, n_near), NEAR, 0, 0, tiled=True)
    return grad_input, slices.reshape(features.shape[1], width)


def solution(mesh):
    fine = Mesh(mesh.devices.reshape(4, 2, 2, 8, 2), ROW + COL)
    placed = (
        P(ROW + COL, None),
        P(ROW + COL, None),
        P(COL + ROW, None),
        P(),
        P(),
        P(),
        P(),
        P(ROW, COL, None, None),
        P(ROW, COL),
        P(ROW, COL),
        P(ROW, COL),
    )
    return jax.shard_map(
        shards,
        mesh=fine,
        in_specs=placed,
        out_specs=(P(COL + ROW, None), P()),
        check_vma=False,
    )
```

```python
import functools

import jax
import jax.numpy as jnp
from jax import lax
from jax.experimental import pallas as pl
from jax.experimental.pallas import tpu as pltpu
from jax.sharding import Mesh, PartitionSpec as P

ROW = ("y", "xl")
COL = ("xh", "z", "c")
NEAR = ROW + ("c",)
FAR = ("xh", "z")
TILE = 128
UNROLL = 4
STAGES = ((0, 1), (2, 3), (4, 5, 6))
VMEM = pl.BlockSpec(memory_space=pltpu.VMEM)
SMEM = pl.BlockSpec(memory_space=pltpu.SMEM)
HBM = pl.BlockSpec(memory_space=pltpu.HBM)
ROOM = pltpu.CompilerParams(vmem_limit_bytes=20 << 20)
TIGHT = pltpu.CompilerParams(vmem_limit_bytes=8 << 20)
F32 = jnp.float32
BF16 = jnp.bfloat16


def mask_kernel(grad_ref, act_ref, out_ref):
    grad = grad_ref[...].astype(F32)
    kept = jnp.where(act_ref[...].astype(F32) > 0, grad, 0.0)
    out_ref[...] = kept.T.astype(BF16)


def turn_kernel(in_ref, out_ref):
    out_ref[...] = in_ref[...].astype(F32).T.astype(BF16)


def table_kernel(
    where_ref,
    count_ref,
    decay_ref,
    rows_ref,
    time_ref,
    degree_ref,
    near_row,
    far_row,
    near_col,
    far_col,
    ends_ref,
    row_time,
    col_time,
    row_scale,
    node_sem,
):
    tile_rows = row_time.shape[0]
    tile_cols = col_time.shape[0]
    row_at = pl.multiple_of(where_ref[0] * tile_rows, 8)
    col_at = pl.multiple_of(where_ref[1] * tile_cols, 8)
    copies = [
        (time_ref.at[pl.ds(row_at, tile_rows)], row_time),
        (time_ref.at[pl.ds(col_at, tile_cols)], col_time),
        (degree_ref.at[pl.ds(row_at, tile_rows)], row_scale),
    ]
    copies = [
        pltpu.make_async_copy(src, dst, node_sem.at[k])
        for k, (src, dst) in enumerate(copies)
    ]
    for copy in copies:
        copy.start()

    xh, z, ring = where_ref[2], where_ref[3], where_ref[5]
    slot = lax.broadcasted_iota(jnp.int32, rows_ref.shape, 1)
    rows = jnp.where(slot < count_ref[0, 0], rows_ref[...], tile_rows)
    half = ring // 2
    here, there = xh * ring, (xh ^ 1) * ring
    last = here + lax.rem(z + half, ring)
    open_at = lax.rem(z + half - 1, ring)
    wrapped = open_at > ring - 3
    shut_at = jnp.where(wrapped, open_at + 3 - ring, open_at + 3)
    chips = (
        (here, last),
        (last + 1, here + ring),
        (there + jnp.where(wrapped, shut_at, 0), there + open_at),
        (there + jnp.where(wrapped, ring, shut_at), there + ring),
        (last, last + 1),
        (there + open_at, there + jnp.where(wrapped, ring, shut_at)),
        (there, there + jnp.where(wrapped, shut_at, 0)),
    )
    for k, pair in enumerate(chips):
        for side, chip in enumerate(pair):
            ends_ref[2 * k + side] = jnp.sum(
                jnp.where(rows < chip * 4, 1, 0).astype(jnp.int32)
            )

    for copy in copies:
        copy.wait()
    decay = decay_ref[0]
    later = decay * row_time[...].astype(F32)
    scale = row_scale[...]
    down = (jnp.exp(-later) * scale).T
    up = (jnp.exp(later) * scale).T
    for row in range(tile_rows):
        near_row[row] = jnp.broadcast_to(down[:, row : row + 1], (TILE, TILE))
        far_row[row] = jnp.broadcast_to(up[:, row : row + 1], (TILE, TILE))
    later = decay * col_time[...].astype(F32)
    near_col[...] = jnp.exp(later).reshape(tile_cols, 1, TILE)
    far_col[...] = jnp.exp(-later).reshape(tile_cols, 1, TILE)


def take_panels(places, blocks, where_ref, panel):
    xh, z, c, ring = (where_ref[k] for k in range(2, 6))
    for (flip, dz, other), block in zip(places, blocks):
        chip = (xh ^ flip) * ring + lax.rem(z + (2 * c - 1) * dz + ring, ring)
        for k in range(block.shape[0]):
            at = chip * 4 + (c ^ other ^ k) * 2
            panel[at] = block[k, :, :TILE]
            panel[at + 1] = block[k, :, TILE:]


def add_slots(ranges, ints, tables, values_ref, panel, total):
    rows_ref, cols_ref = ints
    near_row, far_row, near_col, far_col = tables
    slots = rows_ref.shape[1]
    empty = jnp.zeros((TILE, TILE), BF16)
    lengths = [end - start for start, end in ranges]
    live = sum(lengths)

    def find(place):
        index = jnp.minimum(place, live - 1)
        slot = ranges[0][0] + index
        before = lengths[0]
        for (start, _), length in zip(ranges[1:], lengths[1:]):
            slot = jnp.where(index < before, slot, start + index - before)
            before = before + length
        return slot, jnp.where(place < live, 1.0, 0.0).astype(F32)

    def edges(slot, row, col, inside):
        weight = jnp.minimum(
            near_row[row] * (near_col[col] * inside),
            far_row[row] * (far_col[col] * inside),
        )
        return (values_ref[0, slot].astype(F32) * weight).astype(BF16)

    def group(index, carry):
        parts = []
        for k in range(UNROLL):
            at = index * (2 * UNROLL) + 2 * k
            left, left_in = find(at)
            right, right_in = find(at + 1)
            left_row, left_col = rows_ref[0, left], cols_ref[0, left]
            right_row, right_col = rows_ref[0, right], cols_ref[0, right]
            upper = jnp.concatenate(
                [edges(left, left_row, left_col, left_in), empty], axis=1
            )
            lower = jnp.concatenate(
                [empty, edges(right, right_row, right_col, right_in)], axis=1
            )
            part = jnp.dot(
                jnp.concatenate([panel[left_row], panel[right_row]], axis=1),
                jnp.concatenate([upper, lower], axis=0),
                preferred_element_type=F32,
            )
            parts.append((left_col, right_col, part))
        for left_col, right_col, part in parts:
            total[left_col] += part[:, :TILE]
            total[right_col] += part[:, TILE:]
        return carry

    lax.fori_loop(0, (live + 2 * UNROLL - 1) // (2 * UNROLL), group, 0)


def stage_ranges(ends_ref, stage):
    return [(ends_ref[2 * k], ends_ref[2 * k + 1]) for k in STAGES[stage]]


def early_kernel(stage, places, where_ref, ends_ref, rows_ref, cols_ref, *refs):
    n = len(places)
    values_ref, *tables = refs[n : n + 5]
    *before, total, panel = refs[n + 5 :]
    take_panels(places, refs[:n], where_ref, panel)
    total[...] = before[0][...] if before else jnp.zeros_like(total)
    ranges = stage_ranges(ends_ref, stage)
    add_slots(ranges, (rows_ref, cols_ref), tables, values_ref, panel, total)


def last_kernel(places, spots, where_ref, ends_ref, rows_ref, cols_ref, *refs):
    n, m = len(places), len(spots)
    values_ref, *tables = refs[n + m : n + m + 5]
    before, keep_ref, give_ref, local_ref, panel, total = refs[n + m + 5 :]
    take_panels(places, refs[:n], where_ref, panel)
    total[...] = before[...]
    ranges = stage_ranges(ends_ref, 2)
    add_slots(ranges, (rows_ref, cols_ref), tables, values_ref, panel, total)
    y, xl, reach = (where_ref[k] for k in range(6, 9))
    local = jnp.zeros((panel.shape[1], panel.shape[1]), F32)
    for (dy, flip), feat_ref in zip(spots, refs[n : n + m]):
        at = lax.rem(y + dy + reach, reach)
        owner = at * 2 + (xl ^ flip)
        sums = jnp.concatenate([total[owner * 2], total[owner * 2 + 1]], axis=1)
        high = sums.astype(BF16)
        low = (sums - high.astype(F32)).astype(BF16)
        if flip:
            give_ref[at] = high
        else:
            keep_ref[at] = sums
        for part in (high, low):
            local = local + lax.dot_general(
                feat_ref[flip],
                part,
                (((1,), (1,)), ((), ())),
                preferred_element_type=F32,
            )
    local_ref[...] = local.reshape(local_ref.shape)


def half_kernel(where_ref, keep_ref, got_ref, kept_ref, give_ref):
    y = where_ref[6]
    for k in range(4):
        summed = keep_ref[y ^ k] + got_ref[y ^ k].astype(F32)
        if k < 2:
            kept_ref[k] = summed
        else:
            give_ref[k - 2] = summed.astype(BF16)


def quarter_kernel(keep_ref, got_ref, kept_ref, give_ref):
    kept_ref[...] = keep_ref[0] + got_ref[0].astype(F32)
    give_ref[...] = (keep_ref[1] + got_ref[1].astype(F32)).astype(BF16)


def finish_kernel(weight_ref, keep_ref, got_ref, out_ref):
    summed = keep_ref[...] + got_ref[...].astype(F32)
    out_ref[...] = lax.dot_general(
        summed.T.astype(BF16),
        weight_ref[...],
        (((1,), (1,)), ((), ())),
        preferred_element_type=F32,
    ).astype(BF16)


def spread_kernel(in_ref, out_ref):
    total = in_ref[0].astype(F32)
    for k in range(1, in_ref.shape[0]):
        total = total + in_ref[k].astype(F32)
    total = total.astype(out_ref.dtype)
    for k in range(out_ref.shape[0]):
        out_ref[k] = total


def shift(block, axis, step):
    size = lax.axis_size(axis)
    return lax.ppermute(block, axis, [(i, (i + step) % size) for i in range(size)])


def onward(block):
    ring = lax.axis_size("z")
    pairs = []
    for z in range(ring):
        pairs.append((z * 2, (z + 1) % ring * 2))
        pairs.append((z * 2 + 1, (z - 1) % ring * 2 + 1))
    return lax.ppermute(block, ("z", "c"), pairs)


def gather(own, features, where, turn, make_tables, early):
    tie = lax.optimization_barrier

    def both(flip, step, block):
        return [(flip, step, 0, block), (flip, -step, 1, shift(block, "c", 1))]

    pair = jnp.stack([own, shift(own, "c", 1)])
    other = shift(pair, "xh", 1)
    first, features_t = tie((onward(pair), turn(features)))
    second, other, beside_t = tie(
        (onward(first), other, shift(features_t, "xl", 1))
    )
    second, where = tie((second, where))
    sides = jnp.stack([features_t, beside_t])
    below, above = shift(sides, "y", 1), shift(sides, "y", -1)
    third, other_first, *beside = tie(
        (onward(second), onward(other), *make_tables(where))
    )
    third, below, above = tie((third, below, above))
    near = [(0, 0, 0, pair)] + both(0, 1, first) + both(0, 2, second)
    near += both(0, 3, third)
    fourth = onward(third[:1])
    other_second = onward(other_first)
    other_third = shift(third, "xh", 1)
    total = early(0, near, beside)
    under = shift(below, "y", 1)
    fourth, other_second, under, total = tie((fourth, other_second, under, total))
    other_fourth = shift(fourth, "xh", 1)
    sides = {0: sides, -1: below, 1: above, -2: under}
    far = [(1, 0, 0, other)] + both(1, 1, other_first) + both(1, 2, other_second)
    total = early(1, far, beside, total)
    other_fourth, total = tie((other_fourth, total))
    late = both(0, 4, fourth) + both(1, 3, other_third) + both(1, 4, other_fourth)
    return late, total, beside, sides


def shards(
    out_grad,
    pre_act,
    features,
    weight,
    inv_degree,
    node_time,
    decay_rate,
    tile_value,
    tile_row,
    tile_col,
    tile_count,
):
    nodes, width = out_grad.shape
    slots = tile_value.shape[1]
    n_row = lax.axis_size(ROW)
    n_col = lax.axis_size(COL)
    tile_rows = nodes * n_col // TILE
    tile_cols = nodes * n_row // TILE
    xh, z, c = (lax.axis_index(name) for name in COL)
    where = jnp.stack(
        [lax.axis_index(ROW), lax.axis_index(COL), xh, z, c, lax.axis_size("z")]
        + [lax.axis_index("y"), lax.axis_index("xl"), lax.axis_size("y")]
    ).astype(jnp.int32)

    masked = pl.pallas_call(
        mask_kernel,
        out_shape=jax.ShapeDtypeStruct((width, nodes), BF16),
        in_specs=[VMEM] * 2,
        out_specs=VMEM,
        compiler_params=TIGHT,
    )(out_grad, pre_act)

    def make_tables(where):
        lane = (tile_cols, 1, TILE)
        return pl.pallas_call(
            table_kernel,
            out_shape=(
                jax.ShapeDtypeStruct((tile_rows, TILE, TILE), F32),
                jax.ShapeDtypeStruct((tile_rows, TILE, TILE), F32),
                jax.ShapeDtypeStruct(lane, F32),
                jax.ShapeDtypeStruct(lane, F32),
                jax.ShapeDtypeStruct((14,), jnp.int32),
            ),
            in_specs=[SMEM] * 3 + [VMEM] + [HBM] * 2,
            out_specs=(VMEM,) * 4 + (SMEM,),
            scratch_shapes=[
                pltpu.VMEM((tile_rows, TILE), jnp.int32),
                pltpu.VMEM((tile_cols, TILE), jnp.int32),
                pltpu.VMEM((tile_rows, TILE), F32),
                pltpu.SemaphoreType.DMA((3,)),
            ],
            compiler_params=ROOM,
            cost_estimate=pl.CostEstimate(
                flops=3 * 10**9, bytes_accessed=0, transcendentals=0
            ),
        )(
            where,
            tile_count,
            decay_rate,
            tile_row,
            node_time.reshape(-1, TILE),
            inv_degree.reshape(-1, TILE),
        )

    def turn(array):
        return pl.pallas_call(
            turn_kernel,
            out_shape=jax.ShapeDtypeStruct(array.shape[::-1], BF16),
            in_specs=[VMEM],
            out_specs=VMEM,
            compiler_params=TIGHT,
        )(array)

    def split(found):
        return [place[:3] for place in found], [place[3] for place in found]

    panel = pltpu.VMEM((tile_rows, width, TILE), BF16)
    totals = (tile_cols, width, TILE)

    def early(stage, found, beside, *before):
        places, blocks = split(found)
        *tables, ends = beside
        return pl.pallas_call(
            functools.partial(early_kernel, stage, places),
            out_shape=jax.ShapeDtypeStruct(totals, F32),
            in_specs=[SMEM] * 4 + [VMEM] * (len(blocks) + 5 + len(before)),
            out_specs=VMEM,
            scratch_shapes=[panel],
            compiler_params=ROOM,
            cost_estimate=pl.CostEstimate(
                flops=4 * 10**9, bytes_accessed=0, transcendentals=0
            ),
        )(where, ends, tile_row, tile_col, *blocks, tile_value, *tables, *before)

    late, total, (*tables, ends), sides = gather(
        masked, features, where, turn, make_tables, early
    )
    places, blocks = split(late)
    spots = [(dy, flip) for dy in sides for flip in (0, 1)]
    around = [sides[dy] for dy in sides for flip in (0, 1)]
    n_near = lax.axis_size(NEAR)
    n_far = lax.axis_size(FAR)
    part_rows = features.shape[1] // n_near
    reach = lax.axis_size("y")
    keep, give, local = pl.pallas_call(
        functools.partial(last_kernel, places, spots),
        out_shape=(
            jax.ShapeDtypeStruct((reach, width, nodes), F32),
            jax.ShapeDtypeStruct((reach, width, nodes), BF16),
            jax.ShapeDtypeStruct((n_near, part_rows, width), F32),
        ),
        in_specs=[SMEM] * 4 + [VMEM] * (len(blocks) + len(around) + 6),
        out_specs=(VMEM, VMEM, VMEM),
        scratch_shapes=[panel, pltpu.VMEM(totals, F32)],
        compiler_params=ROOM,
        cost_estimate=pl.CostEstimate(
            flops=4 * 10**9, bytes_accessed=0, transcendentals=0
        ),
    )(
        where,
        ends,
        tile_row,
        tile_col,
        *blocks,
        *around,
        tile_value,
        *tables,
        total,
    )

    def spread(array, copies, dtype):
        return pl.pallas_call(
            spread_kernel,
            out_shape=jax.ShapeDtypeStruct((copies,) + array.shape[1:], dtype),
            in_specs=[VMEM],
            out_specs=VMEM,
            compiler_params=TIGHT,
        )(array)

    got = shift(give, "xl", 1)
    slices = lax.all_to_all(local, NEAR, 0, 0, tiled=True)
    slices, got = lax.optimization_barrier((slices, got))
    block = (2, width, nodes)
    keep, give = pl.pallas_call(
        half_kernel,
        out_shape=(
            jax.ShapeDtypeStruct(block, F32),
            jax.ShapeDtypeStruct(block, BF16),
        ),
        in_specs=[SMEM, VMEM, VMEM],
        out_specs=(VMEM, VMEM),
        compiler_params=TIGHT,
    )(where, keep, got)
    got = shift(give, "y", 2)
    slices = lax.all_to_all(spread(slices, n_far, BF16), FAR, 0, 0, tiled=True)
    slices, got = lax.optimization_barrier((slices, got))
    keep, give = pl.pallas_call(
        quarter_kernel,
        out_shape=(
            jax.ShapeDtypeStruct((width, nodes), F32),
            jax.ShapeDtypeStruct((width, nodes), BF16),
        ),
        in_specs=[VMEM, VMEM],
        out_specs=(VMEM, VMEM),
        compiler_params=TIGHT,
    )(keep, got)
    slices, give = lax.optimization_barrier((spread(slices, n_near, F32), give))
    got = lax.ppermute(give, "y", [(y, y ^ 1) for y in range(reach)])
    grad_input = pl.pallas_call(
        finish_kernel,
        out_shape=jax.ShapeDtypeStruct((nodes, features.shape[1]), BF16),
        in_specs=[VMEM] * 3,
        out_specs=VMEM,
        compiler_params=TIGHT,
    )(weight, keep, got)
    slices = lax.all_to_all(slices, NEAR, 0, 0, tiled=True)
    return grad_input, slices.reshape(features.shape[1], width)


def solution(mesh):
    fine = Mesh(mesh.devices.reshape(4, 2, 2, 8, 2), ROW + COL)
    placed = (
        P(ROW + COL, None),
        P(ROW + COL, None),
        P(COL + ROW, None),
        P(),
        P(),
        P(),
        P(),
        P(ROW, COL, None, None),
        P(ROW, COL),
        P(ROW, COL),
        P(ROW, COL),
    )
    return jax.shard_map(
        shards,
        mesh=fine,
        in_specs=placed,
        out_specs=(P(COL + ROW, None), P()),
        check_vma=False,
    )
```

```python
import functools

import jax
import jax.numpy as jnp
from jax import lax
from jax.experimental import pallas as pl
from jax.experimental.pallas import tpu as pltpu
from jax.sharding import Mesh, PartitionSpec as P

ROW = ("y", "xl")
COL = ("xh", "z", "c")
NEAR = ROW + ("c",)
FAR = ("xh", "z")
TILE = 128
UNROLL = 8
STAGES = ((0, 1), (2, 3), (4, 5, 6))
VMEM = pl.BlockSpec(memory_space=pltpu.VMEM)
SMEM = pl.BlockSpec(memory_space=pltpu.SMEM)
HBM = pl.BlockSpec(memory_space=pltpu.HBM)
ROOM = pltpu.CompilerParams(vmem_limit_bytes=20 << 20)
TIGHT = pltpu.CompilerParams(vmem_limit_bytes=8 << 20)
F32 = jnp.float32
BF16 = jnp.bfloat16


def mask_kernel(grad_ref, act_ref, out_ref):
    grad = grad_ref[...].astype(F32)
    kept = jnp.where(act_ref[...].astype(F32) > 0, grad, 0.0)
    out_ref[...] = kept.T.astype(BF16)


def turn_kernel(in_ref, out_ref):
    out_ref[...] = in_ref[...].astype(F32).T.astype(BF16)


def table_kernel(
    where_ref,
    count_ref,
    decay_ref,
    rows_ref,
    time_ref,
    degree_ref,
    near_row,
    far_row,
    near_col,
    far_col,
    ends_ref,
    row_time,
    col_time,
    row_scale,
    node_sem,
):
    tile_rows = row_time.shape[0]
    tile_cols = col_time.shape[0]
    row_at = pl.multiple_of(where_ref[0] * tile_rows, 8)
    col_at = pl.multiple_of(where_ref[1] * tile_cols, 8)
    copies = [
        (time_ref.at[pl.ds(row_at, tile_rows)], row_time),
        (time_ref.at[pl.ds(col_at, tile_cols)], col_time),
        (degree_ref.at[pl.ds(row_at, tile_rows)], row_scale),
    ]
    copies = [
        pltpu.make_async_copy(src, dst, node_sem.at[k])
        for k, (src, dst) in enumerate(copies)
    ]
    for copy in copies:
        copy.start()

    xh, z, ring = where_ref[2], where_ref[3], where_ref[5]
    slot = lax.broadcasted_iota(jnp.int32, rows_ref.shape, 1)
    rows = jnp.where(slot < count_ref[0, 0], rows_ref[...], tile_rows)
    half = ring // 2
    here, there = xh * ring, (xh ^ 1) * ring
    last = here + lax.rem(z + half, ring)
    open_at = lax.rem(z + half - 1, ring)
    wrapped = open_at > ring - 3
    shut_at = jnp.where(wrapped, open_at + 3 - ring, open_at + 3)
    chips = (
        (here, last),
        (last + 1, here + ring),
        (there + jnp.where(wrapped, shut_at, 0), there + open_at),
        (there + jnp.where(wrapped, ring, shut_at), there + ring),
        (last, last + 1),
        (there + open_at, there + jnp.where(wrapped, ring, shut_at)),
        (there, there + jnp.where(wrapped, shut_at, 0)),
    )
    for k, pair in enumerate(chips):
        for side, chip in enumerate(pair):
            ends_ref[2 * k + side] = jnp.sum(
                jnp.where(rows < chip * 4, 1, 0).astype(jnp.int32)
            )

    for copy in copies:
        copy.wait()
    decay = decay_ref[0]
    later = decay * row_time[...].astype(F32)
    scale = row_scale[...]
    down = (jnp.exp(-later) * scale).T
    up = (jnp.exp(later) * scale).T
    for row in range(tile_rows):
        near_row[row] = jnp.broadcast_to(down[:, row : row + 1], (TILE, TILE))
        far_row[row] = jnp.broadcast_to(up[:, row : row + 1], (TILE, TILE))
    later = decay * col_time[...].astype(F32)
    near_col[...] = jnp.exp(later).reshape(tile_cols, 1, TILE)
    far_col[...] = jnp.exp(-later).reshape(tile_cols, 1, TILE)


def join_kernel(*refs):
    *in_refs, out_ref = refs
    at = 0
    for ref in in_refs:
        block = ref[...].reshape((-1,) + out_ref.shape[1:])
        out_ref[at : at + block.shape[0]] = block
        at += block.shape[0]


def take_panels(places, blocks, where_ref, panel):
    xh, z, c, ring = (where_ref[k] for k in range(2, 6))
    for (other, parts), block in zip(places, blocks):
        for index, part in enumerate(parts):
            if part is None:
                continue
            flip, dz, k = part
            chip = (xh ^ flip) * ring + lax.rem(z + (2 * c - 1) * dz + ring, ring)
            at = chip * 4 + (c ^ other ^ k) * 2
            panel[at] = block[index, :, :TILE]
            panel[at + 1] = block[index, :, TILE:]


def add_slots(ranges, ints, tables, values_ref, panel, total):
    rows_ref, cols_ref = ints
    near_row, far_row, near_col, far_col = tables
    slots = rows_ref.shape[1]
    empty = jnp.zeros((TILE, TILE), BF16)
    lengths = [end - start for start, end in ranges]
    live = sum(lengths)

    def find(place):
        index = jnp.minimum(place, live - 1)
        slot = ranges[0][0] + index
        before = lengths[0]
        for (start, _), length in zip(ranges[1:], lengths[1:]):
            slot = jnp.where(index < before, slot, start + index - before)
            before = before + length
        return slot, jnp.where(place < live, 1.0, 0.0).astype(F32)

    def edges(slot, row, col, inside):
        weight = jnp.minimum(
            near_row[row] * (near_col[col] * inside),
            far_row[row] * (far_col[col] * inside),
        )
        return (values_ref[0, slot].astype(F32) * weight).astype(BF16)

    def group(index, carry):
        parts = []
        for k in range(UNROLL):
            at = index * (2 * UNROLL) + 2 * k
            left, left_in = find(at)
            right, right_in = find(at + 1)
            left_row, left_col = rows_ref[0, left], cols_ref[0, left]
            right_row, right_col = rows_ref[0, right], cols_ref[0, right]
            upper = jnp.concatenate(
                [edges(left, left_row, left_col, left_in), empty], axis=1
            )
            lower = jnp.concatenate(
                [empty, edges(right, right_row, right_col, right_in)], axis=1
            )
            part = jnp.dot(
                jnp.concatenate([panel[left_row], panel[right_row]], axis=1),
                jnp.concatenate([upper, lower], axis=0),
                preferred_element_type=F32,
            )
            parts.append((left_col, right_col, part))
        for left_col, right_col, part in parts:
            total[left_col] += part[:, :TILE]
            total[right_col] += part[:, TILE:]
        return carry

    lax.fori_loop(0, (live + 2 * UNROLL - 1) // (2 * UNROLL), group, 0)


def stage_ranges(ends_ref, stage):
    return [(ends_ref[2 * k], ends_ref[2 * k + 1]) for k in STAGES[stage]]


def early_kernel(stage, places, where_ref, ends_ref, rows_ref, cols_ref, *refs):
    n = len(places)
    values_ref, *tables = refs[n : n + 5]
    *before, total, panel = refs[n + 5 :]
    take_panels(places, refs[:n], where_ref, panel)
    total[...] = before[0][...] if before else jnp.zeros_like(total)
    ranges = stage_ranges(ends_ref, stage)
    add_slots(ranges, (rows_ref, cols_ref), tables, values_ref, panel, total)


def last_kernel(places, spots, where_ref, ends_ref, rows_ref, cols_ref, *refs):
    n, m = len(places), len(spots)
    values_ref, *tables = refs[n + m : n + m + 5]
    before, keep_ref, give_ref, local_ref, panel, total = refs[n + m + 5 :]
    take_panels(places, refs[:n], where_ref, panel)
    total[...] = before[...]
    ranges = stage_ranges(ends_ref, 2)
    add_slots(ranges, (rows_ref, cols_ref), tables, values_ref, panel, total)
    y, xl, reach = (where_ref[k] for k in range(6, 9))
    local = jnp.zeros((panel.shape[1], panel.shape[1]), F32)
    for (dy, flip), feat_ref in zip(spots, refs[n : n + m]):
        at = lax.rem(y + dy + reach, reach)
        owner = at * 2 + (xl ^ flip)
        sums = jnp.concatenate([total[owner * 2], total[owner * 2 + 1]], axis=1)
        high = sums.astype(BF16)
        low = (sums - high.astype(F32)).astype(BF16)
        if flip:
            give_ref[at] = high
        else:
            keep_ref[at] = sums
        for part in (high, low):
            local = local + lax.dot_general(
                feat_ref[flip],
                part,
                (((1,), (1,)), ((), ())),
                preferred_element_type=F32,
            )
    local_ref[...] = local.reshape(local_ref.shape)


def half_kernel(where_ref, keep_ref, got_ref, kept_ref, give_ref):
    y = where_ref[6]
    for k in range(4):
        summed = keep_ref[y ^ k] + got_ref[y ^ k].astype(F32)
        if k < 2:
            kept_ref[k] = summed
        else:
            give_ref[k - 2] = summed.astype(BF16)


def quarter_kernel(keep_ref, got_ref, kept_ref, give_ref):
    kept_ref[...] = keep_ref[0] + got_ref[0].astype(F32)
    give_ref[...] = (keep_ref[1] + got_ref[1].astype(F32)).astype(BF16)


def finish_kernel(weight_ref, keep_ref, got_ref, out_ref):
    summed = keep_ref[...] + got_ref[...].astype(F32)
    out_ref[...] = lax.dot_general(
        summed.T.astype(BF16),
        weight_ref[...],
        (((1,), (1,)), ((), ())),
        preferred_element_type=F32,
    ).astype(BF16)


def spread_kernel(in_ref, out_ref):
    total = in_ref[0].astype(F32)
    for k in range(1, in_ref.shape[0]):
        total = total + in_ref[k].astype(F32)
    total = total.astype(out_ref.dtype)
    for k in range(out_ref.shape[0]):
        out_ref[k] = total


def shift(block, axis, step):
    size = lax.axis_size(axis)
    return lax.ppermute(block, axis, [(i, (i + step) % size) for i in range(size)])


def join(*blocks):
    shape = blocks[0].shape[-2:]
    count = sum(block.size for block in blocks) // (shape[0] * shape[1])
    return pl.pallas_call(
        join_kernel,
        out_shape=jax.ShapeDtypeStruct((count,) + shape, BF16),
        in_specs=[VMEM] * len(blocks),
        out_specs=VMEM,
        compiler_params=TIGHT,
    )(*blocks)


def onward(block):
    ring = lax.axis_size("z")
    pairs = []
    for z in range(ring):
        pairs.append((z * 2, (z + 1) % ring * 2))
        pairs.append((z * 2 + 1, (z - 1) % ring * 2 + 1))
    return lax.ppermute(block, ("z", "c"), pairs)


def gather(own, features, where, turn, make_tables, early):
    tie = lax.optimization_barrier

    def both(block, *parts):
        back = [part and (part[0], -part[1], part[2]) for part in parts]
        return [(0, list(parts), block), (1, back, shift(block, "c", 1))]

    def chip(flip, dz, size=2):
        return [(flip, dz, k) for k in range(size)]

    pair = join(own, shift(own, "c", 1))
    other = shift(pair, "xh", 1)
    first, features_t = tie((onward(pair), turn(features)))
    beside_t = shift(features_t, "xl", 1)
    second, other = tie((onward(first), other))
    third = onward(join(other, second))
    second, where = tie((second, where))
    sides = join(features_t, beside_t)
    below, above = shift(sides, "y", 1), shift(sides, "y", -1)
    firsts, seconds = both(first, *chip(0, 1)), both(second, *chip(0, 2))
    third, below, above, first_back, second_back, *beside = tie(
        (third, below, above, firsts[1][2], seconds[1][2], *make_tables(where))
    )
    fourth = onward(third[:3])
    under = shift(below, "y", 1)
    skip = [None] * 2
    thirds = both(third, *chip(1, 1), *chip(0, 3))
    near = [(0, chip(0, 0), pair), firsts[0], seconds[0]]
    near += [firsts[1][:2] + (first_back,), seconds[1][:2] + (second_back,)]
    near += [(at, skip + parts[2:], block) for at, parts, block in thirds]
    total = early(0, near, beside)
    fourth, under, total = tie((fourth, under, total))
    fifth = onward(fourth[:2])
    crossed = shift(fourth[2:], "xh", 1)
    fourths = both(fourth, *chip(1, 2), *chip(0, 4, 1))
    far = [(0, chip(1, 0), other)]
    far += [(at, parts[:2] + skip, block) for at, parts, block in thirds]
    far += [(at, parts[:2] + [None], block) for at, parts, block in fourths]
    total = early(1, far, beside, total)
    fifth, crossed, total = tie((fifth, crossed, total))
    late = [(at, skip + parts[2:], block) for at, parts, block in fourths]
    late += both(fifth, *chip(1, 3)) + both(crossed, *chip(1, 4, 1))
    return late, total, beside, {0: sides, -1: below, 1: above, -2: under}


def shards(
    out_grad,
    pre_act,
    features,
    weight,
    inv_degree,
    node_time,
    decay_rate,
    tile_value,
    tile_row,
    tile_col,
    tile_count,
):
    nodes, width = out_grad.shape
    slots = tile_value.shape[1]
    n_row = lax.axis_size(ROW)
    n_col = lax.axis_size(COL)
    tile_rows = nodes * n_col // TILE
    tile_cols = nodes * n_row // TILE
    xh, z, c = (lax.axis_index(name) for name in COL)
    where = jnp.stack(
        [lax.axis_index(ROW), lax.axis_index(COL), xh, z, c, lax.axis_size("z")]
        + [lax.axis_index("y"), lax.axis_index("xl"), lax.axis_size("y")]
    ).astype(jnp.int32)

    masked = pl.pallas_call(
        mask_kernel,
        out_shape=jax.ShapeDtypeStruct((width, nodes), BF16),
        in_specs=[VMEM] * 2,
        out_specs=VMEM,
        compiler_params=TIGHT,
    )(out_grad, pre_act)

    def make_tables(where):
        lane = (tile_cols, 1, TILE)
        return pl.pallas_call(
            table_kernel,
            out_shape=(
                jax.ShapeDtypeStruct((tile_rows, TILE, TILE), F32),
                jax.ShapeDtypeStruct((tile_rows, TILE, TILE), F32),
                jax.ShapeDtypeStruct(lane, F32),
                jax.ShapeDtypeStruct(lane, F32),
                jax.ShapeDtypeStruct((14,), jnp.int32),
            ),
            in_specs=[SMEM] * 3 + [VMEM] + [HBM] * 2,
            out_specs=(VMEM,) * 4 + (SMEM,),
            scratch_shapes=[
                pltpu.VMEM((tile_rows, TILE), jnp.int32),
                pltpu.VMEM((tile_cols, TILE), jnp.int32),
                pltpu.VMEM((tile_rows, TILE), F32),
                pltpu.SemaphoreType.DMA((3,)),
            ],
            compiler_params=ROOM,
            cost_estimate=pl.CostEstimate(
                flops=6 * 10**9, bytes_accessed=0, transcendentals=0
            ),
        )(
            where,
            tile_count,
            decay_rate,
            tile_row,
            node_time.reshape(-1, TILE),
            inv_degree.reshape(-1, TILE),
        )

    def turn(array):
        return pl.pallas_call(
            turn_kernel,
            out_shape=jax.ShapeDtypeStruct(array.shape[::-1], BF16),
            in_specs=[VMEM],
            out_specs=VMEM,
            compiler_params=TIGHT,
        )(array)

    def split(found):
        return [place[:2] for place in found], [place[2] for place in found]

    panel = pltpu.VMEM((tile_rows, width, TILE), BF16)
    totals = (tile_cols, width, TILE)

    def early(stage, found, beside, *before):
        places, blocks = split(found)
        *tables, ends = beside
        return pl.pallas_call(
            functools.partial(early_kernel, stage, places),
            out_shape=jax.ShapeDtypeStruct(totals, F32),
            in_specs=[SMEM] * 4 + [VMEM] * (len(blocks) + 5 + len(before)),
            out_specs=VMEM,
            scratch_shapes=[panel],
            compiler_params=ROOM,
            cost_estimate=pl.CostEstimate(
                flops=3 * 10**9, bytes_accessed=0, transcendentals=0
            ),
        )(where, ends, tile_row, tile_col, *blocks, tile_value, *tables, *before)

    late, total, (*tables, ends), sides = gather(
        masked, features, where, turn, make_tables, early
    )
    places, blocks = split(late)
    spots = [(dy, flip) for dy in sides for flip in (0, 1)]
    around = [sides[dy] for dy in sides for flip in (0, 1)]
    n_near = lax.axis_size(NEAR)
    n_far = lax.axis_size(FAR)
    part_rows = features.shape[1] // n_near
    reach = lax.axis_size("y")
    keep, give, local = pl.pallas_call(
        functools.partial(last_kernel, places, spots),
        out_shape=(
            jax.ShapeDtypeStruct((reach, width, nodes), F32),
            jax.ShapeDtypeStruct((reach, width, nodes), BF16),
            jax.ShapeDtypeStruct((n_near, part_rows, width), F32),
        ),
        in_specs=[SMEM] * 4 + [VMEM] * (len(blocks) + len(around) + 6),
        out_specs=(VMEM, VMEM, VMEM),
        scratch_shapes=[panel, pltpu.VMEM(totals, F32)],
        compiler_params=ROOM,
        cost_estimate=pl.CostEstimate(
            flops=3 * 10**9, bytes_accessed=0, transcendentals=0
        ),
    )(
        where,
        ends,
        tile_row,
        tile_col,
        *blocks,
        *around,
        tile_value,
        *tables,
        total,
    )

    def spread(array, copies, dtype):
        return pl.pallas_call(
            spread_kernel,
            out_shape=jax.ShapeDtypeStruct((copies,) + array.shape[1:], dtype),
            in_specs=[VMEM],
            out_specs=VMEM,
            compiler_params=TIGHT,
        )(array)

    got = shift(give, "xl", 1)
    slices = lax.all_to_all(local, NEAR, 0, 0, tiled=True)
    slices, got = lax.optimization_barrier((slices, got))
    block = (2, width, nodes)
    keep, give = pl.pallas_call(
        half_kernel,
        out_shape=(
            jax.ShapeDtypeStruct(block, F32),
            jax.ShapeDtypeStruct(block, BF16),
        ),
        in_specs=[SMEM, VMEM, VMEM],
        out_specs=(VMEM, VMEM),
        compiler_params=TIGHT,
    )(where, keep, got)
    got = shift(give, "y", 2)
    slices = lax.all_to_all(spread(slices, n_far, BF16), FAR, 0, 0, tiled=True)
    keep, give = pl.pallas_call(
        quarter_kernel,
        out_shape=(
            jax.ShapeDtypeStruct((width, nodes), F32),
            jax.ShapeDtypeStruct((width, nodes), BF16),
        ),
        in_specs=[VMEM, VMEM],
        out_specs=(VMEM, VMEM),
        compiler_params=TIGHT,
    )(keep, got)
    got = lax.ppermute(give, "y", [(y, y ^ 1) for y in range(reach)])
    slices, got = lax.optimization_barrier((slices, got))
    grad_input = pl.pallas_call(
        finish_kernel,
        out_shape=jax.ShapeDtypeStruct((nodes, features.shape[1]), BF16),
        in_specs=[VMEM] * 3,
        out_specs=VMEM,
        compiler_params=TIGHT,
    )(weight, keep, got)
    slices = lax.all_to_all(spread(slices, n_near, F32), NEAR, 0, 0, tiled=True)
    return grad_input, slices.reshape(features.shape[1], width)


def solution(mesh):
    fine = Mesh(mesh.devices.reshape(4, 2, 2, 8, 2), ROW + COL)
    placed = (
        P(ROW + COL, None),
        P(ROW + COL, None),
        P(COL + ROW, None),
        P(),
        P(),
        P(),
        P(),
        P(ROW, COL, None, None),
        P(ROW, COL),
        P(ROW, COL),
        P(ROW, COL),
    )
    return jax.shard_map(
        shards,
        mesh=fine,
        in_specs=placed,
        out_specs=(P(COL + ROW, None), P()),
        check_vma=False,
    )
```

```python
import functools

import jax
import jax.numpy as jnp
from jax import lax
from jax.experimental import pallas as pl
from jax.experimental.pallas import tpu as pltpu
from jax.sharding import Mesh, PartitionSpec as P

ROW = ("y", "xl")
COL = ("xh", "z", "c")
NEAR = ROW + ("c",)
FAR = ("xh", "z")
TILE = 128
UNROLL = 8
STAGES = ((0, 1), (2, 3), (4, 5, 6))
VMEM = pl.BlockSpec(memory_space=pltpu.VMEM)
SMEM = pl.BlockSpec(memory_space=pltpu.SMEM)
HBM = pl.BlockSpec(memory_space=pltpu.HBM)
ROOM = pltpu.CompilerParams(vmem_limit_bytes=20 << 20)
TIGHT = pltpu.CompilerParams(vmem_limit_bytes=8 << 20)
F32 = jnp.float32
BF16 = jnp.bfloat16


def mask_kernel(grad_hbm, act_hbm, out_ref, grad_ref, act_ref, sems):
    copies = [
        pltpu.make_async_copy(src, dst, sems.at[k])
        for k, (src, dst) in enumerate(((grad_hbm, grad_ref), (act_hbm, act_ref)))
    ]
    for copy in copies:
        copy.start()
    for copy in copies:
        copy.wait()
    grad = grad_ref[...].astype(F32)
    kept = jnp.where(act_ref[...].astype(F32) > 0, grad, 0.0)
    out_ref[...] = kept.T.astype(BF16)


def turn_kernel(in_ref, out_ref):
    out_ref[...] = in_ref[...].astype(F32).T.astype(BF16)


def table_kernel(
    where_ref,
    count_ref,
    decay_ref,
    rows_hbm,
    time_ref,
    degree_ref,
    near_row,
    far_row,
    near_col,
    far_col,
    ends_ref,
    rows_ref,
    row_time,
    col_time,
    row_scale,
    node_sem,
):
    tile_rows = row_time.shape[0]
    tile_cols = col_time.shape[0]
    row_at = pl.multiple_of(where_ref[0] * tile_rows, 8)
    col_at = pl.multiple_of(where_ref[1] * tile_cols, 8)
    copies = [
        (time_ref.at[pl.ds(row_at, tile_rows)], row_time),
        (time_ref.at[pl.ds(col_at, tile_cols)], col_time),
        (degree_ref.at[pl.ds(row_at, tile_rows)], row_scale),
        (rows_hbm, rows_ref),
    ]
    copies = [
        pltpu.make_async_copy(src, dst, node_sem.at[k])
        for k, (src, dst) in enumerate(copies)
    ]
    for copy in copies:
        copy.start()

    for copy in copies:
        copy.wait()
    xh, z, ring = where_ref[2], where_ref[3], where_ref[5]
    slot = lax.broadcasted_iota(jnp.int32, rows_ref.shape, 1)
    rows = jnp.where(slot < count_ref[0, 0], rows_ref[...], tile_rows)
    half = ring // 2
    here, there = xh * ring, (xh ^ 1) * ring
    last = here + lax.rem(z + half, ring)
    open_at = lax.rem(z + half - 1, ring)
    wrapped = open_at > ring - 3
    shut_at = jnp.where(wrapped, open_at + 3 - ring, open_at + 3)
    chips = (
        (here, last),
        (last + 1, here + ring),
        (there + jnp.where(wrapped, shut_at, 0), there + open_at),
        (there + jnp.where(wrapped, ring, shut_at), there + ring),
        (last, last + 1),
        (there + open_at, there + jnp.where(wrapped, ring, shut_at)),
        (there, there + jnp.where(wrapped, shut_at, 0)),
    )
    for k, pair in enumerate(chips):
        for side, chip in enumerate(pair):
            ends_ref[2 * k + side] = jnp.sum(
                jnp.where(rows < chip * 4, 1, 0).astype(jnp.int32)
            )

    decay = decay_ref[0]
    later = decay * row_time[...].astype(F32)
    scale = row_scale[...]
    down = (jnp.exp(-later) * scale).T
    up = (jnp.exp(later) * scale).T
    for row in range(tile_rows):
        near_row[row] = jnp.broadcast_to(down[:, row : row + 1], (TILE, TILE))
        far_row[row] = jnp.broadcast_to(up[:, row : row + 1], (TILE, TILE))
    later = decay * col_time[...].astype(F32)
    near_col[...] = jnp.exp(later).reshape(tile_cols, 1, TILE)
    far_col[...] = jnp.exp(-later).reshape(tile_cols, 1, TILE)


def join_kernel(*refs):
    *in_refs, out_ref = refs
    at = 0
    for ref in in_refs:
        block = ref[...].reshape((-1,) + out_ref.shape[1:])
        out_ref[at : at + block.shape[0]] = block
        at += block.shape[0]


def take_panels(places, blocks, where_ref, panel):
    xh, z, c, ring = (where_ref[k] for k in range(2, 6))
    for (other, parts), block in zip(places, blocks):
        for index, part in enumerate(parts):
            if part is None:
                continue
            flip, dz, k = part
            chip = (xh ^ flip) * ring + lax.rem(z + (2 * c - 1) * dz + ring, ring)
            at = chip * 4 + (c ^ other ^ k) * 2
            panel[at] = block[index, :, :TILE]
            panel[at + 1] = block[index, :, TILE:]


def add_slots(ranges, ints, tables, values_ref, panel, total):
    rows_ref, cols_ref = ints
    near_row, far_row, near_col, far_col = tables
    slots = rows_ref.shape[1]
    empty = jnp.zeros((TILE, TILE), BF16)
    lengths = [end - start for start, end in ranges]
    live = sum(lengths)

    def find(place):
        index = jnp.minimum(place, live - 1)
        slot = ranges[0][0] + index
        before = lengths[0]
        for (start, _), length in zip(ranges[1:], lengths[1:]):
            slot = jnp.where(index < before, slot, start + index - before)
            before = before + length
        return slot, jnp.where(place < live, 1.0, 0.0).astype(F32)

    def edges(slot, row, col, inside):
        weight = jnp.minimum(
            near_row[row] * (near_col[col] * inside),
            far_row[row] * (far_col[col] * inside),
        )
        return (values_ref[0, slot].astype(F32) * weight).astype(BF16)

    def group(index, carry):
        parts = []
        for k in range(UNROLL):
            at = index * (2 * UNROLL) + 2 * k
            left, left_in = find(at)
            right, right_in = find(at + 1)
            left_row, left_col = rows_ref[0, left], cols_ref[0, left]
            right_row, right_col = rows_ref[0, right], cols_ref[0, right]
            upper = jnp.concatenate(
                [edges(left, left_row, left_col, left_in), empty], axis=1
            )
            lower = jnp.concatenate(
                [empty, edges(right, right_row, right_col, right_in)], axis=1
            )
            part = jnp.dot(
                jnp.concatenate([panel[left_row], panel[right_row]], axis=1),
                jnp.concatenate([upper, lower], axis=0),
                preferred_element_type=F32,
            )
            parts.append((left_col, right_col, part))
        for left_col, right_col, part in parts:
            total[left_col] += part[:, :TILE]
            total[right_col] += part[:, TILE:]
        return carry

    lax.fori_loop(0, (live + 2 * UNROLL - 1) // (2 * UNROLL), group, 0)


def stage_ranges(ends_ref, stage):
    return [(ends_ref[2 * k], ends_ref[2 * k + 1]) for k in STAGES[stage]]


def early_kernel(stage, places, where_ref, ends_ref, rows_ref, cols_ref, *refs):
    n = len(places)
    values_ref, *tables = refs[n : n + 5]
    *before, total, panel = refs[n + 5 :]
    take_panels(places, refs[:n], where_ref, panel)
    total[...] = before[0][...] if before else jnp.zeros_like(total)
    ranges = stage_ranges(ends_ref, stage)
    add_slots(ranges, (rows_ref, cols_ref), tables, values_ref, panel, total)


def last_kernel(places, spots, where_ref, ends_ref, rows_ref, cols_ref, *refs):
    n, m = len(places), len(spots)
    values_ref, *tables = refs[n + m : n + m + 5]
    before, keep_ref, give_ref, local_ref, panel, total = refs[n + m + 5 :]
    take_panels(places, refs[:n], where_ref, panel)
    total[...] = before[...]
    ranges = stage_ranges(ends_ref, 2)
    add_slots(ranges, (rows_ref, cols_ref), tables, values_ref, panel, total)
    y, xl, reach = (where_ref[k] for k in range(6, 9))
    local = jnp.zeros((panel.shape[1], panel.shape[1]), F32)
    for (dy, flip), feat_ref in zip(spots, refs[n : n + m]):
        at = lax.rem(y + dy + reach, reach)
        owner = at * 2 + (xl ^ flip)
        sums = jnp.concatenate([total[owner * 2], total[owner * 2 + 1]], axis=1)
        high = sums.astype(BF16)
        low = (sums - high.astype(F32)).astype(BF16)
        if flip:
            give_ref[at] = high
        else:
            keep_ref[at] = sums
        for part in (high, low):
            local = local + lax.dot_general(
                feat_ref[flip],
                part,
                (((1,), (1,)), ((), ())),
                preferred_element_type=F32,
            )
    local_ref[...] = local.reshape(local_ref.shape)


def half_kernel(where_ref, keep_ref, got_ref, own_ref, *out_refs):
    y, reach = where_ref[6], where_ref[8]
    own_ref[...] = keep_ref[y] + got_ref[y].astype(F32)
    for k, out_ref in enumerate(out_refs):
        at = lax.rem(y + k + 1, reach)
        out_ref[...] = (keep_ref[at] + got_ref[at].astype(F32)).astype(BF16)


def finish_kernel(weight_ref, own_ref, *refs):
    summed = own_ref[...]
    for ref in refs[:-1]:
        summed = summed + ref[...].astype(F32)
    refs[-1][...] = lax.dot_general(
        summed.T.astype(BF16),
        weight_ref[...],
        (((1,), (1,)), ((), ())),
        preferred_element_type=F32,
    ).astype(BF16)


def spread_kernel(in_ref, out_ref):
    total = in_ref[0].astype(F32)
    for k in range(1, in_ref.shape[0]):
        total = total + in_ref[k].astype(F32)
    total = total.astype(out_ref.dtype)
    for k in range(out_ref.shape[0]):
        out_ref[k] = total


def shift(block, axis, step):
    size = lax.axis_size(axis)
    return lax.ppermute(block, axis, [(i, (i + step) % size) for i in range(size)])


def join(*blocks):
    shape = blocks[0].shape[-2:]
    count = sum(block.size for block in blocks) // (shape[0] * shape[1])
    return pl.pallas_call(
        join_kernel,
        out_shape=jax.ShapeDtypeStruct((count,) + shape, BF16),
        in_specs=[VMEM] * len(blocks),
        out_specs=VMEM,
        compiler_params=TIGHT,
    )(*blocks)


def onward(block):
    ring = lax.axis_size("z")
    pairs = []
    for z in range(ring):
        pairs.append((z * 2, (z + 1) % ring * 2))
        pairs.append((z * 2 + 1, (z - 1) % ring * 2 + 1))
    return lax.ppermute(block, ("z", "c"), pairs)


def gather(own, features, where, turn, make_tables, early):
    tie = lax.optimization_barrier

    def both(block, *parts):
        back = [part and (part[0], -part[1], part[2]) for part in parts]
        return [(0, list(parts), block), (1, back, shift(block, "c", 1))]

    def chip(flip, dz, size=2):
        return [(flip, dz, k) for k in range(size)]

    pair = join(own, shift(own, "c", 1))
    other = shift(own, "xh", 1)
    other = join(other, shift(other, "c", 1))
    features_t = turn(features)
    first, beside_t = tie((onward(pair), shift(features_t, "xl", 1)))
    second, other = tie((onward(first), other))
    third = onward(join(other, second))
    second, where = tie((second, where))
    sides = join(features_t, beside_t)
    below, above = shift(sides, "y", 1), shift(sides, "y", -1)
    firsts, seconds = both(first, *chip(0, 1)), both(second, *chip(0, 2))
    third, below, above, first_back, second_back, *beside = tie(
        (third, below, above, firsts[1][2], seconds[1][2], *make_tables(where))
    )
    fourth = onward(third[:3])
    under = shift(below, "y", 1)
    skip = [None] * 2
    thirds = both(third, *chip(1, 1), *chip(0, 3))
    near = [(0, chip(0, 0), pair), firsts[0], seconds[0]]
    near += [firsts[1][:2] + (first_back,), seconds[1][:2] + (second_back,)]
    near += [(at, skip + parts[2:], block) for at, parts, block in thirds]
    total = early(0, near, beside)
    fourth, under, total = tie((fourth, under, total))
    fifth = onward(fourth[:2])
    crossed = shift(fourth[2:], "xh", 1)
    fourths = both(fourth, *chip(1, 2), *chip(0, 4, 1))
    far = [(0, chip(1, 0), other)]
    far += [(at, parts[:2] + skip, block) for at, parts, block in thirds]
    far += [(at, parts[:2] + [None], block) for at, parts, block in fourths]
    total = early(1, far, beside, total)
    fifth, crossed, total = tie((fifth, crossed, total))
    late = [(at, skip + parts[2:], block) for at, parts, block in fourths]
    late += both(fifth, *chip(1, 3)) + both(crossed, *chip(1, 4, 1))
    return late, total, beside, {0: sides, -1: below, 1: above, -2: under}


def shards(
    out_grad,
    pre_act,
    features,
    weight,
    inv_degree,
    node_time,
    decay_rate,
    tile_value,
    tile_row,
    tile_col,
    tile_count,
):
    nodes, width = out_grad.shape
    slots = tile_value.shape[1]
    n_row = lax.axis_size(ROW)
    n_col = lax.axis_size(COL)
    tile_rows = nodes * n_col // TILE
    tile_cols = nodes * n_row // TILE
    xh, z, c = (lax.axis_index(name) for name in COL)
    where = jnp.stack(
        [lax.axis_index(ROW), lax.axis_index(COL), xh, z, c, lax.axis_size("z")]
        + [lax.axis_index("y"), lax.axis_index("xl"), lax.axis_size("y")]
    ).astype(jnp.int32)

    def stay(array):
        return pltpu.with_memory_space_constraint(array, pltpu.HBM)

    masked = pl.pallas_call(
        mask_kernel,
        out_shape=jax.ShapeDtypeStruct((width, nodes), BF16),
        in_specs=[HBM] * 2,
        out_specs=VMEM,
        scratch_shapes=[
            pltpu.VMEM(out_grad.shape, BF16),
            pltpu.VMEM(out_grad.shape, BF16),
            pltpu.SemaphoreType.DMA((2,)),
        ],
        compiler_params=TIGHT,
    )(stay(out_grad), stay(pre_act))

    def make_tables(where):
        lane = (tile_cols, 1, TILE)
        return pl.pallas_call(
            table_kernel,
            out_shape=(
                jax.ShapeDtypeStruct((tile_rows, TILE, TILE), F32),
                jax.ShapeDtypeStruct((tile_rows, TILE, TILE), F32),
                jax.ShapeDtypeStruct(lane, F32),
                jax.ShapeDtypeStruct(lane, F32),
                jax.ShapeDtypeStruct((14,), jnp.int32),
            ),
            in_specs=[SMEM] * 3 + [HBM] * 3,
            out_specs=(VMEM,) * 4 + (SMEM,),
            scratch_shapes=[
                pltpu.VMEM((1, slots), jnp.int32),
                pltpu.VMEM((tile_rows, TILE), jnp.int32),
                pltpu.VMEM((tile_cols, TILE), jnp.int32),
                pltpu.VMEM((tile_rows, TILE), F32),
                pltpu.SemaphoreType.DMA((4,)),
            ],
            compiler_params=ROOM,
            cost_estimate=pl.CostEstimate(
                flops=6 * 10**9, bytes_accessed=0, transcendentals=0
            ),
        )(
            where,
            tile_count,
            decay_rate,
            stay(tile_row),
            stay(node_time.reshape(-1, TILE)),
            stay(inv_degree.reshape(-1, TILE)),
        )

    def turn(array):
        return pl.pallas_call(
            turn_kernel,
            out_shape=jax.ShapeDtypeStruct(array.shape[::-1], BF16),
            in_specs=[VMEM],
            out_specs=VMEM,
            compiler_params=TIGHT,
        )(array)

    def split(found):
        return [place[:2] for place in found], [place[2] for place in found]

    panel = pltpu.VMEM((tile_rows, width, TILE), BF16)
    totals = (tile_cols, width, TILE)

    def early(stage, found, beside, *before):
        places, blocks = split(found)
        *tables, ends = beside
        return pl.pallas_call(
            functools.partial(early_kernel, stage, places),
            out_shape=jax.ShapeDtypeStruct(totals, F32),
            in_specs=[SMEM] * 4 + [VMEM] * (len(blocks) + 5 + len(before)),
            out_specs=VMEM,
            scratch_shapes=[panel],
            compiler_params=ROOM,
            cost_estimate=pl.CostEstimate(
                flops=3 * 10**9, bytes_accessed=0, transcendentals=0
            ),
        )(where, ends, tile_row, tile_col, *blocks, tile_value, *tables, *before)

    late, total, (*tables, ends), sides = gather(
        masked, features, where, turn, make_tables, early
    )
    places, blocks = split(late)
    spots = [(dy, flip) for dy in sides for flip in (0, 1)]
    around = [sides[dy] for dy in sides for flip in (0, 1)]
    n_near = lax.axis_size(NEAR)
    n_far = lax.axis_size(FAR)
    part_rows = features.shape[1] // n_near
    reach = lax.axis_size("y")
    keep, give, local = pl.pallas_call(
        functools.partial(last_kernel, places, spots),
        out_shape=(
            jax.ShapeDtypeStruct((reach, width, nodes), F32),
            jax.ShapeDtypeStruct((reach, width, nodes), BF16),
            jax.ShapeDtypeStruct((n_near, part_rows, width), F32),
        ),
        in_specs=[SMEM] * 4 + [VMEM] * (len(blocks) + len(around) + 6),
        out_specs=(VMEM, VMEM, VMEM),
        scratch_shapes=[panel, pltpu.VMEM(totals, F32)],
        compiler_params=ROOM,
        cost_estimate=pl.CostEstimate(
            flops=3 * 10**9, bytes_accessed=0, transcendentals=0
        ),
    )(
        where,
        ends,
        tile_row,
        tile_col,
        *blocks,
        *around,
        tile_value,
        *tables,
        total,
    )

    def spread(array, copies, dtype):
        return pl.pallas_call(
            spread_kernel,
            out_shape=jax.ShapeDtypeStruct((copies,) + array.shape[1:], dtype),
            in_specs=[VMEM],
            out_specs=VMEM,
            compiler_params=TIGHT,
        )(array)

    got = shift(give, "xl", 1)
    slices = lax.all_to_all(local, NEAR, 0, 0, tiled=True)
    slices, got = lax.optimization_barrier((slices, got))
    block = (width, nodes)
    own, *others = pl.pallas_call(
        half_kernel,
        out_shape=(jax.ShapeDtypeStruct(block, F32),)
        + (jax.ShapeDtypeStruct(block, BF16),) * (reach - 1),
        in_specs=[SMEM, VMEM, VMEM],
        out_specs=(VMEM,) * reach,
        compiler_params=TIGHT,
    )(where, keep, got)
    sent = [shift(other, "y", k + 1) for k, other in enumerate(others)]
    slices = lax.all_to_all(spread(slices, n_far, BF16), FAR, 0, 0, tiled=True)
    grad_input = pl.pallas_call(
        finish_kernel,
        out_shape=jax.ShapeDtypeStruct((nodes, features.shape[1]), BF16),
        in_specs=[VMEM] * (len(sent) + 2),
        out_specs=VMEM,
        cost_estimate=pl.CostEstimate(
            flops=10**10, bytes_accessed=0, transcendentals=0
        ),
        compiler_params=TIGHT,
    )(weight, own, *sent)
    slices = lax.all_to_all(spread(slices, n_near, F32), NEAR, 0, 0, tiled=True)
    return grad_input, slices.reshape(features.shape[1], width)


def solution(mesh):
    fine = Mesh(mesh.devices.reshape(4, 2, 2, 8, 2), ROW + COL)
    placed = (
        P(ROW + COL, None),
        P(ROW + COL, None),
        P(COL + ROW, None),
        P(),
        P(),
        P(),
        P(),
        P(ROW, COL, None, None),
        P(ROW, COL),
        P(ROW, COL),
        P(ROW, COL),
    )
    return jax.shard_map(
        shards,
        mesh=fine,
        in_specs=placed,
        out_specs=(P(COL + ROW, None), P()),
        check_vma=False,
    )
```

```python
import functools

import jax
import jax.numpy as jnp
from jax import lax
from jax.experimental import pallas as pl
from jax.experimental.pallas import tpu as pltpu
from jax.sharding import Mesh, PartitionSpec as P

ROW = ("y", "xl")
COL = ("xh", "z", "c")
NEAR = ROW + ("c",)
FAR = ("xh", "z")
TILE = 128
UNROLL = 8
STAGES = ((0, 1), (2, 3), (4, 5, 6))
VMEM = pl.BlockSpec(memory_space=pltpu.VMEM)
SMEM = pl.BlockSpec(memory_space=pltpu.SMEM)
HBM = pl.BlockSpec(memory_space=pltpu.HBM)
ROOM = pltpu.CompilerParams(vmem_limit_bytes=20 << 20)
TIGHT = pltpu.CompilerParams(vmem_limit_bytes=8 << 20)
F32 = jnp.float32
BF16 = jnp.bfloat16


def mask_kernel(grad_hbm, act_hbm, out_ref, grad_ref, act_ref, sems):
    copies = [
        pltpu.make_async_copy(src, dst, sems.at[k])
        for k, (src, dst) in enumerate(((grad_hbm, grad_ref), (act_hbm, act_ref)))
    ]
    for copy in copies:
        copy.start()
    for copy in copies:
        copy.wait()
    grad = grad_ref[...].astype(F32)
    kept = jnp.where(act_ref[...].astype(F32) > 0, grad, 0.0)
    out_ref[...] = kept.T.astype(BF16)


def turn_kernel(in_ref, out_ref):
    out_ref[...] = in_ref[...].astype(F32).T.astype(BF16)


def table_kernel(
    where_ref,
    count_ref,
    decay_ref,
    rows_hbm,
    time_ref,
    degree_ref,
    near_row,
    far_row,
    near_col,
    far_col,
    ends_ref,
    rows_ref,
    row_time,
    col_time,
    row_scale,
    node_sem,
):
    tile_rows = row_time.shape[0]
    tile_cols = col_time.shape[0]
    row_at = pl.multiple_of(where_ref[0] * tile_rows, 8)
    col_at = pl.multiple_of(where_ref[1] * tile_cols, 8)
    copies = [
        (time_ref.at[pl.ds(row_at, tile_rows)], row_time),
        (time_ref.at[pl.ds(col_at, tile_cols)], col_time),
        (degree_ref.at[pl.ds(row_at, tile_rows)], row_scale),
        (rows_hbm, rows_ref),
    ]
    copies = [
        pltpu.make_async_copy(src, dst, node_sem.at[k])
        for k, (src, dst) in enumerate(copies)
    ]
    for copy in copies:
        copy.start()

    for copy in copies:
        copy.wait()
    xh, z, ring = where_ref[2], where_ref[3], where_ref[5]
    slot = lax.broadcasted_iota(jnp.int32, rows_ref.shape, 1)
    rows = jnp.where(slot < count_ref[0, 0], rows_ref[...], tile_rows)
    half = ring // 2
    here, there = xh * ring, (xh ^ 1) * ring
    last = here + lax.rem(z + half, ring)
    open_at = lax.rem(z + half - 1, ring)
    wrapped = open_at > ring - 3
    shut_at = jnp.where(wrapped, open_at + 3 - ring, open_at + 3)
    chips = (
        (here, last),
        (last + 1, here + ring),
        (there + jnp.where(wrapped, shut_at, 0), there + open_at),
        (there + jnp.where(wrapped, ring, shut_at), there + ring),
        (last, last + 1),
        (there + open_at, there + jnp.where(wrapped, ring, shut_at)),
        (there, there + jnp.where(wrapped, shut_at, 0)),
    )
    for k, pair in enumerate(chips):
        for side, chip in enumerate(pair):
            ends_ref[2 * k + side] = jnp.sum(
                jnp.where(rows < chip * 4, 1, 0).astype(jnp.int32)
            )

    decay = decay_ref[0]
    later = decay * row_time[...].astype(F32)
    scale = row_scale[...]
    down = (jnp.exp(-later) * scale).T
    up = (jnp.exp(later) * scale).T
    for row in range(tile_rows):
        near_row[row] = jnp.broadcast_to(down[:, row : row + 1], (TILE, TILE))
        far_row[row] = jnp.broadcast_to(up[:, row : row + 1], (TILE, TILE))
    later = decay * col_time[...].astype(F32)
    near_col[...] = jnp.exp(later).reshape(tile_cols, 1, TILE)
    far_col[...] = jnp.exp(-later).reshape(tile_cols, 1, TILE)


def join_kernel(*refs):
    *in_refs, out_ref = refs
    at = 0
    for ref in in_refs:
        block = ref[...].reshape((-1,) + out_ref.shape[1:])
        out_ref[at : at + block.shape[0]] = block
        at += block.shape[0]


def take_panels(places, blocks, where_ref, panel):
    xh, z, c, ring = (where_ref[k] for k in range(2, 6))
    for (other, parts), block in zip(places, blocks):
        for index, part in enumerate(parts):
            if part is None:
                continue
            flip, dz, k = part
            chip = (xh ^ flip) * ring + lax.rem(z + (2 * c - 1) * dz + ring, ring)
            at = chip * 4 + (c ^ other ^ k) * 2
            panel[at] = block[index, :, :TILE]
            panel[at + 1] = block[index, :, TILE:]


def add_slots(ranges, ints, tables, values_ref, panel, total):
    rows_ref, cols_ref = ints
    near_row, far_row, near_col, far_col = tables
    slots = rows_ref.shape[1]
    empty = jnp.zeros((TILE, TILE), BF16)
    lengths = [end - start for start, end in ranges]
    live = sum(lengths)

    def find(place):
        index = jnp.minimum(place, live - 1)
        slot = ranges[0][0] + index
        before = lengths[0]
        for (start, _), length in zip(ranges[1:], lengths[1:]):
            slot = jnp.where(index < before, slot, start + index - before)
            before = before + length
        return slot, jnp.where(place < live, 1.0, 0.0).astype(F32)

    def edges(slot, row, col, inside):
        weight = jnp.minimum(
            near_row[row] * (near_col[col] * inside),
            far_row[row] * (far_col[col] * inside),
        )
        return (values_ref[0, slot].astype(F32) * weight).astype(BF16)

    def group(index, carry):
        parts = []
        for k in range(UNROLL):
            at = index * (2 * UNROLL) + 2 * k
            left, left_in = find(at)
            right, right_in = find(at + 1)
            left_row, left_col = rows_ref[0, left], cols_ref[0, left]
            right_row, right_col = rows_ref[0, right], cols_ref[0, right]
            upper = jnp.concatenate(
                [edges(left, left_row, left_col, left_in), empty], axis=1
            )
            lower = jnp.concatenate(
                [empty, edges(right, right_row, right_col, right_in)], axis=1
            )
            part = jnp.dot(
                jnp.concatenate([panel[left_row], panel[right_row]], axis=1),
                jnp.concatenate([upper, lower], axis=0),
                preferred_element_type=F32,
            )
            parts.append((left_col, right_col, part))
        for left_col, right_col, part in parts:
            total[left_col] += part[:, :TILE]
            total[right_col] += part[:, TILE:]
        return carry

    lax.fori_loop(0, (live + 2 * UNROLL - 1) // (2 * UNROLL), group, 0)


def stage_ranges(ends_ref, stage):
    return [(ends_ref[2 * k], ends_ref[2 * k + 1]) for k in STAGES[stage]]


def early_kernel(stage, places, where_ref, ends_ref, rows_ref, cols_ref, *refs):
    n = len(places)
    values_ref, *tables = refs[n : n + 5]
    *before, total, panel = refs[n + 5 :]
    take_panels(places, refs[:n], where_ref, panel)
    total[...] = before[0][...] if before else jnp.zeros_like(total)
    ranges = stage_ranges(ends_ref, stage)
    add_slots(ranges, (rows_ref, cols_ref), tables, values_ref, panel, total)


def last_kernel(places, spots, where_ref, ends_ref, rows_ref, cols_ref, *refs):
    n, m = len(places), len(spots)
    values_ref, *tables = refs[n + m : n + m + 5]
    before, keep_ref, give_ref, local_ref, panel, total = refs[n + m + 5 :]
    take_panels(places, refs[:n], where_ref, panel)
    total[...] = before[...]
    ranges = stage_ranges(ends_ref, 2)
    add_slots(ranges, (rows_ref, cols_ref), tables, values_ref, panel, total)
    y, xl, reach = (where_ref[k] for k in range(6, 9))
    local = jnp.zeros((panel.shape[1], panel.shape[1]), F32)
    for (dy, flip), feat_ref in zip(spots, refs[n : n + m]):
        at = lax.rem(y + dy + reach, reach)
        owner = at * 2 + (xl ^ flip)
        sums = jnp.concatenate([total[owner * 2], total[owner * 2 + 1]], axis=1)
        high = sums.astype(BF16)
        if flip:
            give_ref[at] = high
        else:
            keep_ref[at] = sums
        local = local + lax.dot_general(
            feat_ref[flip],
            high,
            (((1,), (1,)), ((), ())),
            preferred_element_type=F32,
        )
    local_ref[...] = local.astype(BF16).reshape(local_ref.shape)


def half_kernel(where_ref, keep_ref, got_ref, own_ref, *out_refs):
    y, reach = where_ref[6], where_ref[8]
    own_ref[...] = keep_ref[y] + got_ref[y].astype(F32)
    for k, out_ref in enumerate(out_refs):
        at = lax.rem(y + k + 1, reach)
        out_ref[...] = (keep_ref[at] + got_ref[at].astype(F32)).astype(BF16)


def finish_kernel(weight_ref, own_ref, *refs):
    summed = own_ref[...]
    for ref in refs[:-1]:
        summed = summed + ref[...].astype(F32)
    refs[-1][...] = lax.dot_general(
        summed.T.astype(BF16),
        weight_ref[...],
        (((1,), (1,)), ((), ())),
        preferred_element_type=F32,
    ).astype(BF16)


def spread_kernel(in_ref, out_ref):
    total = in_ref[0].astype(F32)
    for k in range(1, in_ref.shape[0]):
        total = total + in_ref[k].astype(F32)
    total = total.astype(out_ref.dtype)
    for k in range(out_ref.shape[0]):
        out_ref[k] = total


def shift(block, axis, step):
    size = lax.axis_size(axis)
    return lax.ppermute(block, axis, [(i, (i + step) % size) for i in range(size)])


def join(*blocks):
    shape = blocks[0].shape[-2:]
    count = sum(block.size for block in blocks) // (shape[0] * shape[1])
    return pl.pallas_call(
        join_kernel,
        out_shape=jax.ShapeDtypeStruct((count,) + shape, BF16),
        in_specs=[VMEM] * len(blocks),
        out_specs=VMEM,
        compiler_params=TIGHT,
    )(*blocks)


def onward(block):
    ring = lax.axis_size("z")
    pairs = []
    for z in range(ring):
        pairs.append((z * 2, (z + 1) % ring * 2))
        pairs.append((z * 2 + 1, (z - 1) % ring * 2 + 1))
    return lax.ppermute(block, ("z", "c"), pairs)


def gather(own, features, where, turn, make_tables, early):
    tie = lax.optimization_barrier

    def both(block, *parts):
        back = [part and (part[0], -part[1], part[2]) for part in parts]
        return [(0, list(parts), block), (1, back, shift(block, "c", 1))]

    def chip(flip, dz, size=2):
        return [(flip, dz, k) for k in range(size)]

    pair = join(own, shift(own, "c", 1))
    other = shift(own, "xh", 1)
    other = join(other, shift(other, "c", 1))
    features_t = turn(features)
    first, beside_t = tie((onward(pair), shift(features_t, "xl", 1)))
    second, other = tie((onward(first), other))
    third = onward(join(other, second))
    second, where = tie((second, where))
    sides = join(features_t, beside_t)
    below, above = shift(sides, "y", 1), shift(sides, "y", -1)
    firsts, seconds = both(first, *chip(0, 1)), both(second, *chip(0, 2))
    third, below, above, first_back, second_back, *beside = tie(
        (third, below, above, firsts[1][2], seconds[1][2], *make_tables(where))
    )
    fourth = onward(third[:3])
    under = shift(below, "y", 1)
    skip = [None] * 2
    thirds = both(third, *chip(1, 1), *chip(0, 3))
    near = [(0, chip(0, 0), pair), firsts[0], seconds[0]]
    near += [firsts[1][:2] + (first_back,), seconds[1][:2] + (second_back,)]
    near += [(at, skip + parts[2:], block) for at, parts, block in thirds]
    total = early(0, near, beside)
    fourth, under, total = tie((fourth, under, total))
    fifth = onward(fourth[:2])
    crossed = shift(fourth[2:], "xh", 1)
    fourths = both(fourth, *chip(1, 2), *chip(0, 4, 1))
    far = [(0, chip(1, 0), other)]
    far += [(at, parts[:2] + skip, block) for at, parts, block in thirds]
    far += [(at, parts[:2] + [None], block) for at, parts, block in fourths]
    total = early(1, far, beside, total)
    fifth, crossed, total = tie((fifth, crossed, total))
    late = [(at, skip + parts[2:], block) for at, parts, block in fourths]
    late += both(fifth, *chip(1, 3)) + both(crossed, *chip(1, 4, 1))
    return late, total, beside, {0: sides, -1: below, 1: above, -2: under}


def shards(
    out_grad,
    pre_act,
    features,
    weight,
    inv_degree,
    node_time,
    decay_rate,
    tile_value,
    tile_row,
    tile_col,
    tile_count,
):
    nodes, width = out_grad.shape
    slots = tile_value.shape[1]
    n_row = lax.axis_size(ROW)
    n_col = lax.axis_size(COL)
    tile_rows = nodes * n_col // TILE
    tile_cols = nodes * n_row // TILE
    xh, z, c = (lax.axis_index(name) for name in COL)
    where = jnp.stack(
        [lax.axis_index(ROW), lax.axis_index(COL), xh, z, c, lax.axis_size("z")]
        + [lax.axis_index("y"), lax.axis_index("xl"), lax.axis_size("y")]
    ).astype(jnp.int32)

    def stay(array):
        return pltpu.with_memory_space_constraint(array, pltpu.HBM)

    masked = pl.pallas_call(
        mask_kernel,
        out_shape=jax.ShapeDtypeStruct((width, nodes), BF16),
        in_specs=[HBM] * 2,
        out_specs=VMEM,
        scratch_shapes=[
            pltpu.VMEM(out_grad.shape, BF16),
            pltpu.VMEM(out_grad.shape, BF16),
            pltpu.SemaphoreType.DMA((2,)),
        ],
        compiler_params=TIGHT,
    )(stay(out_grad), stay(pre_act))

    def make_tables(where):
        lane = (tile_cols, 1, TILE)
        return pl.pallas_call(
            table_kernel,
            out_shape=(
                jax.ShapeDtypeStruct((tile_rows, TILE, TILE), F32),
                jax.ShapeDtypeStruct((tile_rows, TILE, TILE), F32),
                jax.ShapeDtypeStruct(lane, F32),
                jax.ShapeDtypeStruct(lane, F32),
                jax.ShapeDtypeStruct((14,), jnp.int32),
            ),
            in_specs=[SMEM] * 3 + [HBM] * 3,
            out_specs=(VMEM,) * 4 + (SMEM,),
            scratch_shapes=[
                pltpu.VMEM((1, slots), jnp.int32),
                pltpu.VMEM((tile_rows, TILE), jnp.int32),
                pltpu.VMEM((tile_cols, TILE), jnp.int32),
                pltpu.VMEM((tile_rows, TILE), F32),
                pltpu.SemaphoreType.DMA((4,)),
            ],
            compiler_params=ROOM,
            cost_estimate=pl.CostEstimate(
                flops=6 * 10**9, bytes_accessed=0, transcendentals=0
            ),
        )(
            where,
            tile_count,
            decay_rate,
            stay(tile_row),
            stay(node_time.reshape(-1, TILE)),
            stay(inv_degree.reshape(-1, TILE)),
        )

    def turn(array):
        return pl.pallas_call(
            turn_kernel,
            out_shape=jax.ShapeDtypeStruct(array.shape[::-1], BF16),
            in_specs=[VMEM],
            out_specs=VMEM,
            compiler_params=TIGHT,
        )(array)

    def split(found):
        return [place[:2] for place in found], [place[2] for place in found]

    panel = pltpu.VMEM((tile_rows, width, TILE), BF16)
    totals = (tile_cols, width, TILE)

    def early(stage, found, beside, *before):
        places, blocks = split(found)
        *tables, ends = beside
        return pl.pallas_call(
            functools.partial(early_kernel, stage, places),
            out_shape=jax.ShapeDtypeStruct(totals, F32),
            in_specs=[SMEM] * 4 + [VMEM] * (len(blocks) + 5 + len(before)),
            out_specs=VMEM,
            scratch_shapes=[panel],
            compiler_params=ROOM,
            cost_estimate=pl.CostEstimate(
                flops=3 * 10**9, bytes_accessed=0, transcendentals=0
            ),
        )(where, ends, tile_row, tile_col, *blocks, tile_value, *tables, *before)

    late, total, (*tables, ends), sides = gather(
        masked, features, where, turn, make_tables, early
    )
    places, blocks = split(late)
    spots = [(dy, flip) for dy in sides for flip in (0, 1)]
    around = [sides[dy] for dy in sides for flip in (0, 1)]
    n_near = lax.axis_size(NEAR)
    n_far = lax.axis_size(FAR)
    part_rows = features.shape[1] // n_near
    reach = lax.axis_size("y")
    keep, give, local = pl.pallas_call(
        functools.partial(last_kernel, places, spots),
        out_shape=(
            jax.ShapeDtypeStruct((reach, width, nodes), F32),
            jax.ShapeDtypeStruct((reach, width, nodes), BF16),
            jax.ShapeDtypeStruct((n_near, part_rows, width), BF16),
        ),
        in_specs=[SMEM] * 4 + [VMEM] * (len(blocks) + len(around) + 6),
        out_specs=(VMEM, VMEM, VMEM),
        scratch_shapes=[panel, pltpu.VMEM(totals, F32)],
        compiler_params=ROOM,
        cost_estimate=pl.CostEstimate(
            flops=3 * 10**9, bytes_accessed=0, transcendentals=0
        ),
    )(
        where,
        ends,
        tile_row,
        tile_col,
        *blocks,
        *around,
        tile_value,
        *tables,
        total,
    )

    def spread(array, copies, dtype):
        return pl.pallas_call(
            spread_kernel,
            out_shape=jax.ShapeDtypeStruct((copies,) + array.shape[1:], dtype),
            in_specs=[VMEM],
            out_specs=VMEM,
            compiler_params=TIGHT,
        )(array)

    got = shift(give, "xl", 1)
    slices = lax.all_to_all(local, NEAR, 0, 0, tiled=True)
    slices, got = lax.optimization_barrier((slices, got))
    block = (width, nodes)
    own, *others = pl.pallas_call(
        half_kernel,
        out_shape=(jax.ShapeDtypeStruct(block, F32),)
        + (jax.ShapeDtypeStruct(block, BF16),) * (reach - 1),
        in_specs=[SMEM, VMEM, VMEM],
        out_specs=(VMEM,) * reach,
        compiler_params=TIGHT,
    )(where, keep, got)
    sent = [shift(other, "y", k + 1) for k, other in enumerate(others)]
    slices = lax.all_to_all(spread(slices, n_far, BF16), FAR, 0, 0, tiled=True)
    grad_input = pl.pallas_call(
        finish_kernel,
        out_shape=jax.ShapeDtypeStruct((nodes, features.shape[1]), BF16),
        in_specs=[VMEM] * (len(sent) + 2),
        out_specs=VMEM,
        cost_estimate=pl.CostEstimate(
            flops=10**10, bytes_accessed=0, transcendentals=0
        ),
        compiler_params=TIGHT,
    )(weight, own, *sent)
    slices = lax.all_to_all(spread(slices, n_near, F32), NEAR, 0, 0, tiled=True)
    return grad_input, slices.reshape(features.shape[1], width)


def solution(mesh):
    fine = Mesh(mesh.devices.reshape(4, 2, 2, 8, 2), ROW + COL)
    placed = (
        P(ROW + COL, None),
        P(ROW + COL, None),
        P(COL + ROW, None),
        P(),
        P(),
        P(),
        P(),
        P(ROW, COL, None, None),
        P(ROW, COL),
        P(ROW, COL),
        P(ROW, COL),
    )
    return jax.shard_map(
        shards,
        mesh=fine,
        in_specs=placed,
        out_specs=(P(COL + ROW, None), P()),
        check_vma=False,
    )
```

```python
import functools

import jax
import jax.numpy as jnp
from jax import lax
from jax.experimental import pallas as pl
from jax.experimental.pallas import tpu as pltpu
from jax.sharding import Mesh, PartitionSpec as P

ROW = ("y", "xl")
COL = ("xh", "z", "c")
NEAR = ROW + ("c",)
FAR = ("xh", "z")
TILE = 128
UNROLL = 8
STAGES = ((0, 1), (2, 3), (4, 5, 6))
VMEM = pl.BlockSpec(memory_space=pltpu.VMEM)
SMEM = pl.BlockSpec(memory_space=pltpu.SMEM)
HBM = pl.BlockSpec(memory_space=pltpu.HBM)
ROOM = pltpu.CompilerParams(vmem_limit_bytes=20 << 20)
TIGHT = pltpu.CompilerParams(vmem_limit_bytes=8 << 20)
F32 = jnp.float32
BF16 = jnp.bfloat16


def mask_kernel(grad_hbm, act_hbm, out_ref, grad_ref, act_ref, sems):
    copies = [
        pltpu.make_async_copy(src, dst, sems.at[k])
        for k, (src, dst) in enumerate(((grad_hbm, grad_ref), (act_hbm, act_ref)))
    ]
    for copy in copies:
        copy.start()
    for copy in copies:
        copy.wait()
    grad = grad_ref[...].astype(F32)
    kept = jnp.where(act_ref[...].astype(F32) > 0, grad, 0.0)
    out_ref[...] = kept.T.astype(BF16)


def turn_kernel(in_ref, out_ref):
    out_ref[...] = in_ref[...].astype(F32).T.astype(BF16)


def table_kernel(
    where_ref,
    count_ref,
    decay_ref,
    rows_hbm,
    time_ref,
    degree_ref,
    near_row,
    far_row,
    near_col,
    far_col,
    ends_ref,
    rows_ref,
    row_time,
    col_time,
    row_scale,
    node_sem,
):
    tile_rows = row_time.shape[0]
    tile_cols = col_time.shape[0]
    row_at = pl.multiple_of(where_ref[0] * tile_rows, 8)
    col_at = pl.multiple_of(where_ref[1] * tile_cols, 8)
    copies = [
        (time_ref.at[pl.ds(row_at, tile_rows)], row_time),
        (time_ref.at[pl.ds(col_at, tile_cols)], col_time),
        (degree_ref.at[pl.ds(row_at, tile_rows)], row_scale),
        (rows_hbm, rows_ref),
    ]
    copies = [
        pltpu.make_async_copy(src, dst, node_sem.at[k])
        for k, (src, dst) in enumerate(copies)
    ]
    for copy in copies:
        copy.start()

    for copy in copies:
        copy.wait()
    xh, z, ring = where_ref[2], where_ref[3], where_ref[5]
    slot = lax.broadcasted_iota(jnp.int32, rows_ref.shape, 1)
    rows = jnp.where(slot < count_ref[0, 0], rows_ref[...], tile_rows)
    half = ring // 2
    here, there = xh * ring, (xh ^ 1) * ring
    last = here + lax.rem(z + half, ring)
    open_at = lax.rem(z + half - 1, ring)
    wrapped = open_at > ring - 3
    shut_at = jnp.where(wrapped, open_at + 3 - ring, open_at + 3)
    chips = (
        (here, last),
        (last + 1, here + ring),
        (there + jnp.where(wrapped, shut_at, 0), there + open_at),
        (there + jnp.where(wrapped, ring, shut_at), there + ring),
        (last, last + 1),
        (there + open_at, there + jnp.where(wrapped, ring, shut_at)),
        (there, there + jnp.where(wrapped, shut_at, 0)),
    )
    for k, pair in enumerate(chips):
        for side, chip in enumerate(pair):
            ends_ref[2 * k + side] = jnp.sum(
                jnp.where(rows < chip * 4, 1, 0).astype(jnp.int32)
            )

    decay = decay_ref[0]
    later = decay * row_time[...].astype(F32)
    scale = row_scale[...]
    down = (jnp.exp(-later) * scale).T
    up = (jnp.exp(later) * scale).T
    for row in range(tile_rows):
        near_row[row] = jnp.broadcast_to(down[:, row : row + 1], (TILE, TILE))
        far_row[row] = jnp.broadcast_to(up[:, row : row + 1], (TILE, TILE))
    later = decay * col_time[...].astype(F32)
    near_col[...] = jnp.exp(later).reshape(tile_cols, 1, TILE)
    far_col[...] = jnp.exp(-later).reshape(tile_cols, 1, TILE)


def join_kernel(*refs):
    *in_refs, out_ref = refs
    at = 0
    for ref in in_refs:
        block = ref[...].reshape((-1,) + out_ref.shape[1:])
        out_ref[at : at + block.shape[0]] = block
        at += block.shape[0]


def take_panels(places, blocks, where_ref, panel):
    xh, z, c, ring = (where_ref[k] for k in range(2, 6))
    for (other, parts), block in zip(places, blocks):
        for index, part in enumerate(parts):
            if part is None:
                continue
            flip, dz, k = part
            chip = (xh ^ flip) * ring + lax.rem(z + (2 * c - 1) * dz + ring, ring)
            at = chip * 4 + (c ^ other ^ k) * 2
            panel[at] = block[index, :, :TILE]
            panel[at + 1] = block[index, :, TILE:]


def add_slots(ranges, ints, tables, values_ref, panel, total):
    rows_ref, cols_ref = ints
    near_row, far_row, near_col, far_col = tables
    slots = rows_ref.shape[1]
    empty = jnp.zeros((TILE, TILE), BF16)
    lengths = [end - start for start, end in ranges]
    live = sum(lengths)

    def find(place):
        index = jnp.minimum(place, live - 1)
        slot = ranges[0][0] + index
        before = lengths[0]
        for (start, _), length in zip(ranges[1:], lengths[1:]):
            slot = jnp.where(index < before, slot, start + index - before)
            before = before + length
        return slot, jnp.where(place < live, 1.0, 0.0).astype(F32)

    def edges(slot, row, col, inside):
        weight = jnp.minimum(
            near_row[row] * (near_col[col] * inside),
            far_row[row] * (far_col[col] * inside),
        )
        return (values_ref[0, slot].astype(F32) * weight).astype(BF16)

    def group(index, carry):
        parts = []
        for k in range(UNROLL):
            at = index * (2 * UNROLL) + 2 * k
            left, left_in = find(at)
            right, right_in = find(at + 1)
            left_row, left_col = rows_ref[0, left], cols_ref[0, left]
            right_row, right_col = rows_ref[0, right], cols_ref[0, right]
            upper = jnp.concatenate(
                [edges(left, left_row, left_col, left_in), empty], axis=1
            )
            lower = jnp.concatenate(
                [empty, edges(right, right_row, right_col, right_in)], axis=1
            )
            part = jnp.dot(
                jnp.concatenate([panel[left_row], panel[right_row]], axis=1),
                jnp.concatenate([upper, lower], axis=0),
                preferred_element_type=F32,
            )
            parts.append((left_col, right_col, part))
        for left_col, right_col, part in parts:
            total[left_col] += part[:, :TILE]
            total[right_col] += part[:, TILE:]
        return carry

    lax.fori_loop(0, (live + 2 * UNROLL - 1) // (2 * UNROLL), group, 0)


def stage_ranges(ends_ref, stage):
    return [(ends_ref[2 * k], ends_ref[2 * k + 1]) for k in STAGES[stage]]


def early_kernel(stage, places, where_ref, ends_ref, rows_ref, cols_ref, *refs):
    n = len(places)
    values_ref, *tables = refs[n : n + 5]
    *before, total, panel = refs[n + 5 :]
    take_panels(places, refs[:n], where_ref, panel)
    total[...] = before[0][...] if before else jnp.zeros_like(total)
    ranges = stage_ranges(ends_ref, stage)
    add_slots(ranges, (rows_ref, cols_ref), tables, values_ref, panel, total)


def last_kernel(places, spots, where_ref, ends_ref, rows_ref, cols_ref, *refs):
    n, m = len(places), len(spots)
    values_ref, *tables = refs[n + m : n + m + 5]
    before, keep_ref, give_ref, local_ref, panel, total = refs[n + m + 5 :]
    take_panels(places, refs[:n], where_ref, panel)
    total[...] = before[...]
    ranges = stage_ranges(ends_ref, 2)
    add_slots(ranges, (rows_ref, cols_ref), tables, values_ref, panel, total)
    y, xl, reach = (where_ref[k] for k in range(6, 9))
    local = jnp.zeros((panel.shape[1], panel.shape[1]), F32)
    for (dy, flip), feat_ref in zip(spots, refs[n : n + m]):
        at = lax.rem(y + dy + reach, reach)
        owner = at * 2 + (xl ^ flip)
        sums = jnp.concatenate([total[owner * 2], total[owner * 2 + 1]], axis=1)
        high = sums.astype(BF16)
        if flip:
            give_ref[at] = high
        else:
            keep_ref[at] = sums
        local = local + lax.dot_general(
            feat_ref[flip],
            high,
            (((1,), (1,)), ((), ())),
            preferred_element_type=F32,
        )
    local_ref[...] = local.astype(BF16).reshape(local_ref.shape)


def half_kernel(where_ref, keep_ref, got_ref, own_ref, *out_refs):
    y, reach = where_ref[6], where_ref[8]
    own_ref[...] = keep_ref[y] + got_ref[y].astype(F32)
    for k, out_ref in enumerate(out_refs):
        at = lax.rem(y + k + 1, reach)
        out_ref[...] = (keep_ref[at] + got_ref[at].astype(F32)).astype(BF16)


def finish_kernel(weight_ref, own_ref, *refs):
    summed = own_ref[...]
    for ref in refs[:-1]:
        summed = summed + ref[...].astype(F32)
    refs[-1][...] = lax.dot_general(
        summed.T.astype(BF16),
        weight_ref[...],
        (((1,), (1,)), ((), ())),
        preferred_element_type=F32,
    ).astype(BF16)


def spread_kernel(in_ref, out_ref):
    total = in_ref[0].astype(F32)
    for k in range(1, in_ref.shape[0]):
        total = total + in_ref[k].astype(F32)
    total = total.astype(out_ref.dtype)
    for k in range(out_ref.shape[0]):
        out_ref[k] = total


def shift(block, axis, step):
    size = lax.axis_size(axis)
    return lax.ppermute(block, axis, [(i, (i + step) % size) for i in range(size)])


def join(*blocks):
    shape = blocks[0].shape[-2:]
    count = sum(block.size for block in blocks) // (shape[0] * shape[1])
    return pl.pallas_call(
        join_kernel,
        out_shape=jax.ShapeDtypeStruct((count,) + shape, BF16),
        in_specs=[VMEM] * len(blocks),
        out_specs=VMEM,
        compiler_params=TIGHT,
    )(*blocks)


def onward(block):
    ring = lax.axis_size("z")
    pairs = []
    for z in range(ring):
        pairs.append((z * 2, (z + 1) % ring * 2))
        pairs.append((z * 2 + 1, (z - 1) % ring * 2 + 1))
    return lax.ppermute(block, ("z", "c"), pairs)


def gather(own, features, where, turn, make_tables, early):
    tie = lax.optimization_barrier

    def both(block, *parts):
        back = [part and (part[0], -part[1], part[2]) for part in parts]
        return [(0, list(parts), block), (1, back, shift(block, "c", 1))]

    def chip(flip, dz, size=2):
        return [(flip, dz, k) for k in range(size)]

    pair = join(own, shift(own, "c", 1))
    other = shift(own, "xh", 1)
    other = join(other, shift(other, "c", 1))
    features_t = turn(features)
    first, beside_t = tie((onward(pair), shift(features_t, "xl", 1)))
    second, other = tie((onward(first), other))
    third = onward(join(other, second))
    second, where = tie((second, where))
    sides = join(features_t, beside_t)
    below, above = shift(sides, "y", 1), shift(sides, "y", -1)
    firsts, seconds = both(first, *chip(0, 1)), both(second, *chip(0, 2))
    third, below, above, first_back, second_back, *beside = tie(
        (third, below, above, firsts[1][2], seconds[1][2], *make_tables(where))
    )
    fourth = onward(third[:3])
    under = shift(below, "y", 1)
    skip = [None] * 2
    thirds = both(third, *chip(1, 1), *chip(0, 3))
    near = [(0, chip(0, 0), pair), firsts[0], seconds[0]]
    near += [firsts[1][:2] + (first_back,), seconds[1][:2] + (second_back,)]
    near += [(at, skip + parts[2:], block) for at, parts, block in thirds]
    total = early(0, near, beside)
    fourth, under, total = tie((fourth, under, total))
    fifth = onward(fourth[:2])
    crossed = shift(fourth[2:], "xh", 1)
    fourths = both(fourth, *chip(1, 2), *chip(0, 4, 1))
    far = [(0, chip(1, 0), other)]
    far += [(at, parts[:2] + skip, block) for at, parts, block in thirds]
    far += [(at, parts[:2] + [None], block) for at, parts, block in fourths]
    total = early(1, far, beside, total)
    fifth, crossed, total = tie((fifth, crossed, total))
    late = [(at, skip + parts[2:], block) for at, parts, block in fourths]
    late += both(fifth, *chip(1, 3)) + both(crossed, *chip(1, 4, 1))
    return late, total, beside, {0: sides, -1: below, 1: above, -2: under}


def shards(
    out_grad,
    pre_act,
    features,
    weight,
    inv_degree,
    node_time,
    decay_rate,
    tile_value,
    tile_row,
    tile_col,
    tile_count,
):
    nodes, width = out_grad.shape
    slots = tile_value.shape[1]
    n_row = lax.axis_size(ROW)
    n_col = lax.axis_size(COL)
    tile_rows = nodes * n_col // TILE
    tile_cols = nodes * n_row // TILE
    xh, z, c = (lax.axis_index(name) for name in COL)
    where = jnp.stack(
        [lax.axis_index(ROW), lax.axis_index(COL), xh, z, c, lax.axis_size("z")]
        + [lax.axis_index("y"), lax.axis_index("xl"), lax.axis_size("y")]
    ).astype(jnp.int32)

    def stay(array):
        return pltpu.with_memory_space_constraint(array, pltpu.HBM)

    masked = pl.pallas_call(
        mask_kernel,
        out_shape=jax.ShapeDtypeStruct((width, nodes), BF16),
        in_specs=[HBM] * 2,
        out_specs=VMEM,
        scratch_shapes=[
            pltpu.VMEM(out_grad.shape, BF16),
            pltpu.VMEM(out_grad.shape, BF16),
            pltpu.SemaphoreType.DMA((2,)),
        ],
        compiler_params=TIGHT,
    )(stay(out_grad), stay(pre_act))

    def make_tables(where):
        lane = (tile_cols, 1, TILE)
        return pl.pallas_call(
            table_kernel,
            out_shape=(
                jax.ShapeDtypeStruct((tile_rows, TILE, TILE), F32),
                jax.ShapeDtypeStruct((tile_rows, TILE, TILE), F32),
                jax.ShapeDtypeStruct(lane, F32),
                jax.ShapeDtypeStruct(lane, F32),
                jax.ShapeDtypeStruct((14,), jnp.int32),
            ),
            in_specs=[SMEM] * 3 + [HBM] * 3,
            out_specs=(VMEM,) * 4 + (SMEM,),
            scratch_shapes=[
                pltpu.VMEM((1, slots), jnp.int32),
                pltpu.VMEM((tile_rows, TILE), jnp.int32),
                pltpu.VMEM((tile_cols, TILE), jnp.int32),
                pltpu.VMEM((tile_rows, TILE), F32),
                pltpu.SemaphoreType.DMA((4,)),
            ],
            compiler_params=ROOM,
            cost_estimate=pl.CostEstimate(
                flops=6 * 10**9, bytes_accessed=0, transcendentals=0
            ),
        )(
            where,
            tile_count,
            decay_rate,
            stay(tile_row),
            stay(node_time.reshape(-1, TILE)),
            stay(inv_degree.reshape(-1, TILE)),
        )

    def turn(array):
        return pl.pallas_call(
            turn_kernel,
            out_shape=jax.ShapeDtypeStruct(array.shape[::-1], BF16),
            in_specs=[VMEM],
            out_specs=VMEM,
            compiler_params=TIGHT,
        )(array)

    def split(found):
        return [place[:2] for place in found], [place[2] for place in found]

    panel = pltpu.VMEM((tile_rows, width, TILE), BF16)
    totals = (tile_cols, width, TILE)

    def early(stage, found, beside, *before):
        places, blocks = split(found)
        *tables, ends = beside
        return pl.pallas_call(
            functools.partial(early_kernel, stage, places),
            out_shape=jax.ShapeDtypeStruct(totals, F32),
            in_specs=[SMEM] * 4 + [VMEM] * (len(blocks) + 5 + len(before)),
            out_specs=VMEM,
            scratch_shapes=[panel],
            compiler_params=ROOM,
            cost_estimate=pl.CostEstimate(
                flops=3 * 10**9, bytes_accessed=0, transcendentals=0
            ),
        )(where, ends, tile_row, tile_col, *blocks, tile_value, *tables, *before)

    late, total, (*tables, ends), sides = gather(
        masked, features, where, turn, make_tables, early
    )
    places, blocks = split(late)
    spots = [(dy, flip) for dy in sides for flip in (0, 1)]
    around = [sides[dy] for dy in sides for flip in (0, 1)]
    n_near = lax.axis_size(NEAR)
    n_far = lax.axis_size(FAR)
    part_rows = features.shape[1] // n_near
    reach = lax.axis_size("y")
    keep, give, local = pl.pallas_call(
        functools.partial(last_kernel, places, spots),
        out_shape=(
            jax.ShapeDtypeStruct((reach, width, nodes), F32),
            jax.ShapeDtypeStruct((reach, width, nodes), BF16),
            jax.ShapeDtypeStruct((n_near, part_rows, width), BF16),
        ),
        in_specs=[SMEM] * 4 + [VMEM] * (len(blocks) + len(around) + 6),
        out_specs=(VMEM, VMEM, VMEM),
        scratch_shapes=[panel, pltpu.VMEM(totals, F32)],
        compiler_params=ROOM,
        cost_estimate=pl.CostEstimate(
            flops=3 * 10**9, bytes_accessed=0, transcendentals=0
        ),
    )(
        where,
        ends,
        tile_row,
        tile_col,
        *blocks,
        *around,
        tile_value,
        *tables,
        total,
    )

    def spread(array, copies, dtype):
        return pl.pallas_call(
            spread_kernel,
            out_shape=jax.ShapeDtypeStruct((copies,) + array.shape[1:], dtype),
            in_specs=[VMEM],
            out_specs=VMEM,
            compiler_params=TIGHT,
        )(array)

    got = shift(give, "xl", 1)
    slices = lax.all_to_all(local, NEAR, 0, 0, tiled=True)
    slices, got = lax.optimization_barrier((slices, got))
    block = (width, nodes)
    own, *others = pl.pallas_call(
        half_kernel,
        out_shape=(jax.ShapeDtypeStruct(block, F32),)
        + (jax.ShapeDtypeStruct(block, BF16),) * (reach - 1),
        in_specs=[SMEM, VMEM, VMEM],
        out_specs=(VMEM,) * reach,
        compiler_params=TIGHT,
    )(where, keep, got)
    sent = [shift(other, "y", k + 1) for k, other in enumerate(others)]
    slices = lax.all_to_all(spread(slices, n_far, BF16), FAR, 0, 0, tiled=True)
    grad_input = pl.pallas_call(
        finish_kernel,
        out_shape=jax.ShapeDtypeStruct((nodes, features.shape[1]), BF16),
        in_specs=[VMEM] * (len(sent) + 2),
        out_specs=VMEM,
        cost_estimate=pl.CostEstimate(
            flops=10**10, bytes_accessed=0, transcendentals=0
        ),
        compiler_params=TIGHT,
    )(weight, own, *sent)
    slices = lax.all_to_all(spread(slices, n_near, BF16), NEAR, 0, 0, tiled=True)
    return grad_input, slices.reshape(features.shape[1], width).astype(F32)


def solution(mesh):
    fine = Mesh(mesh.devices.reshape(4, 2, 2, 8, 2), ROW + COL)
    placed = (
        P(ROW + COL, None),
        P(ROW + COL, None),
        P(COL + ROW, None),
        P(),
        P(),
        P(),
        P(),
        P(ROW, COL, None, None),
        P(ROW, COL),
        P(ROW, COL),
        P(ROW, COL),
    )
    return jax.shard_map(
        shards,
        mesh=fine,
        in_specs=placed,
        out_specs=(P(COL + ROW, None), P()),
        check_vma=False,
    )
```
